32 devices in a mesh: dp: 4 (over x, core), seq: 8 (over z, y).
Axes of the slice: x: 2, y: 2, z: 4, core: 2. Of those that a mesh axis runs over, the one named last changes fastest.
Arguments:
- qkv: bfloat16 [3, 4, 1024, 16, 128], P(None, 'dp', 'seq'), may hold values from -6 to 6
- tile_mask: int32 [8, 8, 8], replicated, may hold values from 0 to 1, as said below
- d_out: bfloat16 [4, 1024, 3072], P('dp', 'seq'), may hold values from -6 to 6
- w_out: bfloat16 [16, 128, 3072], P('seq'), may hold values from -0.109375 to 0.109375
- momentum: float32 [16, 128, 3072], P('seq'), may hold values from -170 to 170
Outputs:
- grad_qkv: bfloat16 [3, 4, 1024, 16, 128], P(None, 'dp', 'seq')
- synced_momentum: bfloat16 [16, 128, 3072], P('seq')
- worker_error: float32 [4, 16, 128, 3072], P('dp', 'seq')
- server_error: float32 [16, 128, 3072], P('seq', 'dp')
The draws below stay inside these ranges and needn't reach their ends.
Inputs may be any that keep to these rules, and one draw needn't show every extreme that they name: tile_mask[g, i, j] is 1 exactly when tiles i and j, numbered frame by frame over 2 frames of 2 by 2 tiles, differ by at most a per-group reach in frames (0 to 2), in tile rows (0 or 1) and in tile columns (0 or 1); every tile sees itself.
All inputs are finite; a program needn't handle non-finite values. Where the reference program divides by a largest or mean magnitude, that divisor is 1e-20 or more.
Results may differ from the reference program's by a relative error of at most 0.0085.
Values may be sent and summed in bfloat16 or wider, within the bound.
No kernel may reach another device: no remote copies, remote signals or barrier semaphores. Data moves between devices by JAX's collectives and lax.ppermute only.
A program may use at most 128 MiB of HBM per device.

```python
import math
import jax
import jax.numpy as jnp
from jax import lax

D = 3072
HEADS = 16
HEAD_DIM = 128
GROUPS = 8
TILE = 128
LENGTH = 1024
TILES = 8
SEQS = 4


def draw_qkv(key, part):
    values = jnp.clip(jax.random.normal(key, (3, SEQS, LENGTH, HEADS, HEAD_DIM), jnp.float32), -4.0, 4.0)
    return values.astype(jnp.bfloat16)


def draw_tile_mask(key, part):
    frame_reach = jax.random.randint(jax.random.fold_in(key, 21), (GROUPS,), 0, 3)
    row_reach = jax.random.randint(jax.random.fold_in(key, 22), (GROUPS,), 0, 2)
    column_reach = jax.random.randint(jax.random.fold_in(key, 23), (GROUPS,), 0, 2)
    tile_ids = jnp.arange(TILES)
    frame = tile_ids // 4
    tile_row = tile_ids % 4 // 2
    tile_column = tile_ids % 2
    near_frame = jnp.abs(frame[:, None] - frame[None, :])[None] <= frame_reach[:, None, None]
    near_row = jnp.abs(tile_row[:, None] - tile_row[None, :])[None] <= row_reach[:, None, None]
    near_column = jnp.abs(tile_column[:, None] - tile_column[None, :])[None] <= column_reach[:, None, None]
    return (near_frame & near_row & near_column).astype(jnp.int32)


def draw_momentum(key, part):
    noise = jnp.clip(jax.random.normal(key, (HEADS, HEAD_DIM, D), jnp.float32), -4.0, 4.0)
    row_scale = jnp.exp(jax.random.uniform(jax.random.fold_in(key, 31), (HEADS, HEAD_DIM, 1), jnp.float32, 0.0, math.log(10.0)))
    column_scale = jnp.exp(jax.random.uniform(jax.random.fold_in(key, 32), (1, 1, D), jnp.float32, 0.0, math.log(3.0)))
    return noise * row_scale * column_scale


def level_of(stream_key, extent, pieces, least, top_value):
    def one(position, shards_of):
        steps = jax.random.uniform(jax.random.fold_in(jax.random.fold_in(stream_key, 6), position), (shards_of,), jnp.float32, least / len(pieces), top_value / len(pieces))
        return jnp.repeat(jnp.exp(steps), extent[position] // shards_of).reshape((-1,) + (1,) * (len(extent) - position - 1))

    factor_of = one(*pieces[0])
    for cut in pieces[1:]:
        factor_of = factor_of * one(*cut)
    return factor_of


def gaussian(rng, dims, scale, limit, cuts=(), kind=jnp.bfloat16):
    values = scale * jax.random.normal(rng, dims, jnp.float32)
    if cuts:
        values = values * level_of(rng, dims, cuts, -0.22, 0.18)
    return jnp.clip(values, -limit, limit).astype(kind)


def setup_inputs(seed: int = 0) -> dict:
    splits = jax.random.split(jax.random.key(seed), 6)
    qkv = draw_qkv(jax.random.fold_in(splits[5], 71), 0)
    tile_mask = draw_tile_mask(jax.random.fold_in(splits[5], 71), 0)
    d_out = gaussian(splits[2], (SEQS, LENGTH, D), 1.0, 6.0, ((0, 4), (1, 8)))
    w_out = gaussian(splits[3], (HEADS, HEAD_DIM, D), D ** -0.5, 0.109375, ((0, 8),))
    momentum = draw_momentum(jax.random.fold_in(splits[5], 71), 0)
    return dict(qkv=qkv, tile_mask=tile_mask, d_out=d_out, w_out=w_out, momentum=momentum)


def one_head(inputs):
    query_head, key_head, value_head, cot_head, head_tiles = inputs
    inv_root = 1.0 / math.sqrt(HEAD_DIM)
    scores = jnp.dot(query_head, key_head.T, preferred_element_type=jnp.float32) * inv_root
    visible = jnp.repeat(jnp.repeat(head_tiles, TILE, axis=0), TILE, axis=1) > 0
    scores = jnp.where(visible, scores, -jnp.inf)
    row_top = lax.optimization_barrier(jnp.max(scores, axis=-1, keepdims=True))
    expo = jnp.exp(scores - row_top)
    probs = expo / lax.optimization_barrier(jnp.sum(expo, axis=-1, keepdims=True))
    probs_b = probs.astype(jnp.bfloat16)
    attended = jnp.dot(probs_b, value_head, preferred_element_type=jnp.float32).astype(jnp.bfloat16)
    delta = lax.optimization_barrier(jnp.sum(cot_head.astype(jnp.float32) * attended.astype(jnp.float32), axis=-1))
    grad_v = jnp.dot(probs_b.T, cot_head, preferred_element_type=jnp.float32).astype(jnp.bfloat16)
    dprobs = jnp.dot(cot_head, value_head.T, preferred_element_type=jnp.float32)
    dscores = (probs * (dprobs - delta[:, None])).astype(jnp.bfloat16)
    grad_q = (jnp.dot(dscores, key_head, preferred_element_type=jnp.float32) * inv_root).astype(jnp.bfloat16)
    grad_k = (jnp.dot(dscores.T, query_head, preferred_element_type=jnp.float32) * inv_root).astype(jnp.bfloat16)
    return (attended, grad_q, grad_k, grad_v)

def reference(qkv, tile_mask, d_out, w_out, momentum):
    group_of_head = jnp.arange(HEADS) // (HEADS // GROUPS)
    head_masks = tile_mask[group_of_head]

    def one_sequence(inputs):
        triple, cot_rows = inputs
        head_cot = jnp.einsum('ld,hed->lhe', cot_rows.astype(jnp.float32), w_out.astype(jnp.float32)).astype(jnp.bfloat16)
        attended, grad_q, grad_k, grad_v = lax.map(one_head, (jnp.transpose(triple[0], (1, 0, 2)), jnp.transpose(triple[1], (1, 0, 2)), jnp.transpose(triple[2], (1, 0, 2)), jnp.transpose(head_cot, (1, 0, 2)), head_masks))
        grad_weight = jnp.einsum('hle,ld->hed', attended.astype(jnp.float32), cot_rows.astype(jnp.float32))
        grads = jnp.transpose(jnp.stack([grad_q, grad_k, grad_v]), (0, 2, 1, 3))
        return (grads, grad_weight)
    grads, grad_weight = lax.map(one_sequence, (jnp.transpose(qkv, (1, 0, 2, 3, 4)), d_out))
    grad_qkv = jnp.transpose(grads, (1, 0, 2, 3, 4))
    worker_mom = 0.9 * momentum[None] + 0.1 * grad_weight
    worker_scale = lax.optimization_barrier(jnp.mean(jnp.abs(worker_mom), axis=(2, 3), keepdims=True)) + 1e-06
    sent = (worker_scale * jnp.tanh(worker_mom / worker_scale)).astype(jnp.bfloat16)
    worker_error = worker_mom - sent.astype(jnp.float32)
    averaged = lax.optimization_barrier(jnp.sum(sent.astype(jnp.float32), axis=0)) / SEQS
    blocks = averaged.reshape(HEADS, SEQS, HEAD_DIM // SEQS, D)
    server_scale = lax.optimization_barrier(jnp.mean(jnp.abs(blocks), axis=(2, 3), keepdims=True)) + 1e-06
    synced = (server_scale * jnp.tanh(blocks / server_scale)).astype(jnp.bfloat16)
    server_error = (blocks - synced.astype(jnp.float32)).reshape(HEADS, HEAD_DIM, D)
    return (grad_qkv, synced.reshape(HEADS, HEAD_DIM, D), worker_error, server_error)
```

```python
import functools
import math

import jax
import jax.numpy as jnp
from jax import lax
from jax.experimental import pallas as pl
from jax.experimental.pallas import tpu as pltpu
from jax.sharding import PartitionSpec as P

VMEM_LIMIT = 44 * 1024 * 1024
F32 = jnp.float32
BF16 = jnp.bfloat16


def params():
    return pltpu.CompilerParams(vmem_limit_bytes=VMEM_LIMIT)


def cost(flops, moved):
    return pl.CostEstimate(flops=flops, bytes_accessed=moved, transcendentals=0)


def ring_order(n):
    return [i for i in range(n) if i % 2 == 0] + [i for i in reversed(range(n)) if i % 2]


def ring_member(place, n):
    return jnp.where(place < n // 2, 2 * place, 2 * n - 1 - 2 * place)


def ring_place(member, n):
    return jnp.where(member % 2 == 0, member // 2, (2 * n - 1 - member) // 2)


def dot_nt(a, b):
    return lax.dot_general(a, b, (((1,), (1,)), ((), ())), preferred_element_type=F32)


def dot_tn(a, b):
    return lax.dot_general(a, b, (((0,), (0,)), ((), ())), preferred_element_type=F32)


def pack_kernel(n, x_ref, *refs):
    outs, parts = refs[:n], refs[n]
    me = lax.axis_index("seq")
    rows, heads, size = x_ref.shape
    wide = heads * size // n
    x = x_ref[...].reshape(rows, heads * size)
    for d in range(n):
        parts[d] = x[:, d * wide : (d + 1) * wide]
    for k in range(n):
        outs[k][...] = parts[me ^ k]


def unpack_kernel(n, *refs):
    blocks, out_ref, parts = refs[:n], refs[n], refs[n + 1]
    me = lax.axis_index("seq")
    for k in range(n):
        parts[me ^ k] = blocks[k][...]
    out_ref[...] = jnp.concatenate([parts[d] for d in range(n)], axis=1).reshape(out_ref.shape)


def attend_kernel(n, heads_here, per_group, groups, offsets, pieces, first, last, *refs):
    refs = list(refs)
    count = len(offsets)
    take = lambda m: [refs.pop(0) for _ in range(m)]
    (mask_ref,) = take(1)
    tiles = [take(pieces) for _ in range(count)]
    (w_ref,) = take(1)
    blocks = take(n)
    if not first:
        key_in, value_in = take(2)
    if not first and not last:
        (weight_in,) = take(1)
    if last:
        query_parts = take(2)
        outs = take(n)
        (att_ref,) = take(1)
    else:
        query_out, key_out, value_out, weight_out = take(4)
    q_all, k_all, v_all, cot_all, att_all, tile_ids = take(6)
    if last:
        key_out, value_out, grads, query_out = take(4)

    me = lax.axis_index("seq")
    tokens = blocks[0].shape[0] // 3
    wide = blocks[0].shape[1]
    size = wide // heads_here
    inv_root = 1.0 / math.sqrt(size)
    place = ring_place(me, n)
    for i, offset in enumerate(offsets):
        tile_ids[i] = ring_member(lax.rem(place + offset + n, n), n)
    for k in range(n):
        rows = slice(k * tokens, (k + 1) * tokens)
        q_all[k] = blocks[k][0:tokens]
        k_all[rows] = blocks[k][tokens : 2 * tokens]
        v_all[rows] = blocks[k][2 * tokens : 3 * tokens]
    for i in range(count):
        part = tokens // pieces
        for j in range(pieces):
            cot_all[i, j * part : (j + 1) * part] = dot_nt(tiles[i][j][...], w_ref[...]).astype(BF16)
    if first:
        key_out[...] = jnp.zeros_like(key_out)
        value_out[...] = jnp.zeros_like(value_out)
    else:
        key_out[...] = key_in[...]
        value_out[...] = value_in[...]

    def one_tile(i, carry):
        tile = tile_ids[i]
        slot = tile ^ me
        for h in range(heads_here):
            cols = slice(h * size, (h + 1) * size)
            group = (me * heads_here + h) // per_group
            base = (group * n + tile) * n
            bias = jnp.concatenate(
                [
                    jnp.full(
                        (1, tokens), jnp.where(mask_ref[base + (me ^ k)] == 1, 0.0, -jnp.inf), F32
                    )
                    for k in range(n)
                ],
                axis=1,
            )
            query = q_all[slot, :, cols]
            keys = k_all[:, cols]
            values = v_all[:, cols]
            cot = cot_all[i, :, cols]
            scores = dot_nt(query, keys) * inv_root + bias
            expo = jnp.exp(scores - jnp.max(scores, axis=1, keepdims=True))
            probs = expo * (1.0 / jnp.sum(expo, axis=1, keepdims=True))
            probs_b = probs.astype(BF16)
            att = jnp.dot(probs_b, values, preferred_element_type=F32).astype(BF16)
            att_all[i, :, cols] = att
            delta = jnp.sum(cot.astype(F32) * att.astype(F32), axis=1, keepdims=True)
            dprobs = dot_nt(cot, values)
            dscores = (probs * (dprobs - delta)).astype(BF16)
            query_out[i, :, cols] = (
                jnp.dot(dscores, keys, preferred_element_type=F32) * inv_root
            ).astype(BF16)
            key_out[:, cols] += dot_tn(dscores, query)
            value_out[:, cols] += dot_tn(probs_b, cot)
        return carry

    if count == 1:
        one_tile(0, 0)
    else:
        lax.fori_loop(0, count, one_tile, 0)

    if last:
        att_ref[...] = att_all[0]
        for part, listed in zip(query_parts, LISTED(n)):
            for i, offset in enumerate(listed):
                tile = ring_member(lax.rem(place + offset + n, n), n)
                grads[tile ^ me, 0:tokens] = part[i]
        grads[tile_ids[0] ^ me, 0:tokens] = query_out[0]
        for k in range(n):
            rows = slice(k * tokens, (k + 1) * tokens)
            outs[k][0:tokens] = grads[k, 0:tokens]
            outs[k][tokens : 2 * tokens] = (key_out[rows] * inv_root).astype(BF16)
            outs[k][2 * tokens : 3 * tokens] = value_out[rows].astype(BF16)
    else:
        wide_d = w_ref.shape[1]
        chunk = math.gcd(wide_d, 512)
        for c in range(0, wide_d, chunk):
            cols = slice(c, c + chunk)
            total = None if first else weight_in[:, cols]
            for i in range(count):
                term = dot_tn(att_all[i], tiles[i][0][:, cols])
                total = term if total is None else total + term
            weight_out[:, cols] = total


def LISTED(n):
    half = n // 2
    early = [0] + [o for s in range(1, half - 1) for o in (-s, s)]
    return early, [-(half - 1), half - 1]


def worker_kernel(heads_here, workers, mom_ref, weight_ref, att_ref, *refs):
    pieces, error_ref, outs, sent_ref = refs[:-workers - 2], refs[-workers - 2], refs[-workers - 1 : -1], refs[-1]
    me = lax.axis_index("dp")
    tokens, wide = att_ref.shape
    size = wide // heads_here
    wide_d = mom_ref.shape[1]
    chunk = math.gcd(wide_d, 512)
    part = tokens // len(pieces)
    totals = [jnp.zeros((size, chunk), F32) for _ in range(heads_here)]
    for c in range(0, wide_d, chunk):
        cols = slice(c, c + chunk)
        tile = jnp.concatenate([p[:, cols] for p in pieces], axis=0)
        grad = weight_ref[:, cols] + dot_tn(att_ref[...], tile)
        mom = 0.9 * mom_ref[:, cols] + 0.1 * grad
        error_ref[:, cols] = mom
        for h in range(heads_here):
            totals[h] = totals[h] + jnp.abs(mom[h * size : (h + 1) * size])
    for h in range(heads_here):
        rows = slice(h * size, (h + 1) * size)
        scale = jnp.sum(totals[h], keepdims=True) * (1.0 / (size * wide_d)) + 1e-06
        inverse = 1.0 / scale
        for c in range(0, wide_d, chunk):
            cols = slice(c, c + chunk)
            mom = error_ref[rows, cols]
            sent = (scale * jnp.tanh(mom * inverse)).astype(BF16)
            sent_ref[h, :, cols] = sent
            error_ref[rows, cols] = mom - sent.astype(F32)
    block = size // workers
    for k in range(workers):
        start = pl.multiple_of((me ^ k) * block, block)
        outs[k][...] = sent_ref[:, pl.ds(start, block), :]


def server_kernel(workers, *refs):
    blocks, synced_ref, error_ref = refs[:workers], refs[workers], refs[workers + 1]
    heads_here, block, wide_d = synced_ref.shape
    for h in range(heads_here):
        total = blocks[0][h].astype(F32)
        for k in range(1, workers):
            total = total + blocks[k][h].astype(F32)
        averaged = total * (1.0 / workers)
        scale = jnp.sum(jnp.abs(averaged), keepdims=True) * (1.0 / (block * wide_d)) + 1e-06
        synced = (scale * jnp.tanh(averaged * (1.0 / scale))).astype(BF16)
        synced_ref[h] = synced
        error_ref[h] = averaged - synced.astype(F32)


def join_kernel(workers, *refs):
    blocks, out_ref = refs[:workers], refs[workers]
    me = lax.axis_index("dp")
    block = blocks[0].shape[1]
    for k in range(workers):
        start = pl.multiple_of((me ^ k) * block, block)
        out_ref[:, pl.ds(start, block), :] = blocks[k][...]


def body(qkv, tile_mask, d_out, w_out, momentum):
    n = lax.axis_size("seq")
    workers = lax.axis_size("dp")
    tokens, heads, size = qkv.shape[2:]
    heads_here = w_out.shape[0]
    groups = tile_mask.shape[0]
    per_group = heads // groups
    wide = heads_here * size
    wide_d = d_out.shape[2]
    half = n // 2
    shape = jax.ShapeDtypeStruct

    ring = ring_order(n)
    ahead = [(ring[i], ring[(i + 1) % n]) for i in range(n)]
    back = [(b, a) for a, b in ahead]
    own = d_out[0]
    fore, aft = [own], [own]
    for s in range(1, half):
        fore.append(lax.ppermute(fore[-1], "seq", ahead))
        aft.append(lax.ppermute(aft[-1], "seq", back))
    far = [
        lax.ppermute(fore[-1][: tokens // 2], "seq", ahead),
        lax.ppermute(aft[-1][tokens // 2 :], "seq", back),
    ]

    packed = pl.pallas_call(
        functools.partial(pack_kernel, n),
        out_shape=[shape((3 * tokens, wide), BF16)] * n,
        scratch_shapes=[pltpu.VMEM((n, 3 * tokens, wide), BF16)],
        compiler_params=params(),
        cost_estimate=cost(0, 4 * qkv.size),
        name="pack",
    )(qkv.reshape(3 * tokens, heads, size))

    def swap(blocks, axis):
        return [blocks[0]] + [
            lax.ppermute(blocks[k], axis, [(i, i ^ k) for i in range(len(blocks))])
            for k in range(1, len(blocks))
        ]

    blocks = swap(packed, "seq")
    mask = tile_mask.reshape(-1)
    w_flat = w_out.reshape(wide, wide_d)
    early, late = LISTED(n)
    vmem = pl.BlockSpec(memory_space=pltpu.VMEM)
    smem = pl.BlockSpec(memory_space=pltpu.SMEM)
    length = n * tokens

    def attend(offsets, tiles, carried, last=False, parts=()):
        count, pieces = len(offsets), len(tiles[0])
        first = not carried
        pair = [shape((length, wide), F32)] * 2
        operands = [mask, *[p for t in tiles for p in t], w_flat, *blocks, *carried, *parts]
        if last:
            outs = [shape((3 * tokens, wide), BF16)] * n + [shape((tokens, wide), BF16)]
        else:
            outs = [shape((count, tokens, wide), BF16), *pair, shape((wide, wide_d), F32)]
        scratch = [
            pltpu.VMEM((n, tokens, wide), BF16),
            pltpu.VMEM((length, wide), BF16),
            pltpu.VMEM((length, wide), BF16),
            pltpu.VMEM((count, tokens, wide), BF16),
            pltpu.VMEM((count, tokens, wide), BF16),
            pltpu.SMEM((count,), jnp.int32),
        ]
        if last:
            scratch += [
                pltpu.VMEM((length, wide), F32),
                pltpu.VMEM((length, wide), F32),
                pltpu.VMEM((n, tokens, wide), BF16),
                pltpu.VMEM((1, tokens, wide), BF16),
            ]
        flops = count * (14 * tokens * length * wide + 4 * tokens * wide * wide_d)
        return pl.pallas_call(
            functools.partial(
                attend_kernel, n, heads_here, per_group, groups, offsets, pieces, first, last
            ),
            in_specs=[smem] + [vmem] * (len(operands) - 1),
            out_shape=outs,
            scratch_shapes=scratch,
            compiler_params=params(),
            cost_estimate=cost(flops, 2**23),
            name="attend",
        )(*operands)

    by_offset = {0: own}
    for s in range(1, half):
        by_offset[-s], by_offset[s] = fore[s], aft[s]
    query_a, key_a, value_a, weight_a = attend(early, [[by_offset[o]] for o in early], [])
    query_b, key_b, value_b, weight_b = attend(
        late, [[by_offset[o]] for o in late], [key_a, value_a, weight_a]
    )
    *grads, att = attend([half], [far], [key_b, value_b], True, [query_a, query_b])
    returned = swap(grads, "seq")

    error, *sent = pl.pallas_call(
        functools.partial(worker_kernel, heads_here, workers),
        out_shape=[shape((wide, wide_d), F32)]
        + [shape((heads_here, size // workers, wide_d), BF16)] * workers,
        scratch_shapes=[pltpu.VMEM((heads_here, size, wide_d), BF16)],
        compiler_params=params(),
        cost_estimate=cost(2 * tokens * wide * wide_d, 2**24),
        name="worker",
    )(momentum.reshape(wide, wide_d), weight_b, att, *far)
    received = swap(sent, "dp")

    synced, server_error = pl.pallas_call(
        functools.partial(server_kernel, workers),
        out_shape=[
            shape((heads_here, size // workers, wide_d), BF16),
            shape((heads_here, size // workers, wide_d), F32),
        ],
        compiler_params=params(),
        cost_estimate=cost(0, 2**22),
        name="server",
    )(*received)
    gathered = [synced] + [None] * (workers - 1)
    for k in range(1, workers):
        source, step = (synced, k) if k == 1 or k % 2 == 0 else (gathered[k - 1], 1)
        gathered[k] = lax.ppermute(source, "dp", [(i, i ^ step) for i in range(workers)])

    grad_rows = pl.pallas_call(
        functools.partial(unpack_kernel, n),
        out_shape=shape((3 * tokens, heads, size), BF16),
        scratch_shapes=[pltpu.VMEM((n, 3 * tokens, wide), BF16)],
        compiler_params=params(),
        cost_estimate=cost(0, 4 * qkv.size),
        name="unpack",
    )(*returned)
    synced_momentum = pl.pallas_call(
        functools.partial(join_kernel, workers),
        out_shape=shape((heads_here, size, wide_d), BF16),
        compiler_params=params(),
        cost_estimate=cost(0, 4 * w_out.size),
        name="join",
    )(*gathered)
    return (
        grad_rows.reshape(qkv.shape),
        synced_momentum,
        error.reshape(1, heads_here, size, wide_d),
        server_error,
    )


def solution(mesh):
    placed = (
        P(None, "dp", "seq", None, None),
        P(),
        P("dp", "seq", None),
        P("seq", None, None),
        P("seq", None, None),
    )
    return jax.shard_map(
        body,
        mesh=mesh,
        in_specs=placed,
        out_specs=(
            P(None, "dp", "seq", None, None),
            P("seq", None, None),
            P("dp", "seq", None, None),
            P("seq", "dp", None),
        ),
        check_vma=False,
    )
```

```python
import functools
import math

import jax
import jax.numpy as jnp
from jax import lax
from jax.experimental import pallas as pl
from jax.experimental.pallas import tpu as pltpu
from jax.sharding import PartitionSpec as P

SMALL, LARGE = 16 * 1024 * 1024, 60 * 1024 * 1024
F32 = jnp.float32
BF16 = jnp.bfloat16


def params(limit):
    return pltpu.CompilerParams(vmem_limit_bytes=limit)


def cost(flops, moved):
    return pl.CostEstimate(flops=flops, bytes_accessed=moved, transcendentals=0)


def ring_order(n):
    return [i for i in range(n) if i % 2 == 0] + [i for i in reversed(range(n)) if i % 2]


def ring_member(place, n):
    return jnp.where(place < n // 2, 2 * place, 2 * n - 1 - 2 * place)


def ring_place(member, n):
    return jnp.where(member % 2 == 0, member // 2, (2 * n - 1 - member) // 2)


def dot_nt(a, b):
    return lax.dot_general(a, b, (((1,), (1,)), ((), ())), preferred_element_type=F32)


def dot_tn(a, b):
    return lax.dot_general(a, b, (((0,), (0,)), ((), ())), preferred_element_type=F32)


def pack_kernel(n, x_ref, out_ref):
    rows, heads, size = x_ref.shape
    wide = heads * size // n
    x = x_ref[...].reshape(rows, heads * size)
    for d in range(n):
        out_ref[d] = x[:, d * wide : (d + 1) * wide]


def unpack_kernel(n, blocks, out_ref):
    out_ref[...] = jnp.concatenate([blocks[d] for d in range(n)], axis=1).reshape(out_ref.shape)


def fetch(copies, sems, first=0):
    started = [
        pltpu.make_async_copy(source, target, sems.at[first + i])
        for i, (source, target) in enumerate(copies)
    ]
    for copy in started:
        copy.start()
    return started


def rows_of(tiles, buffer):
    copies, start = [], 0
    for tile in tiles:
        copies.append((tile, buffer.at[pl.ds(start, tile.shape[0])]))
        start += tile.shape[0]
    return copies


def attend_kernel(n, heads_here, per_group, groups, first, earlier, mask_ref, *refs):
    refs = list(refs)
    last = earlier is not None
    count = sum(len(g) for g in groups)
    take = lambda m: [refs.pop(0) for _ in range(m)]
    tiles = take(count)
    w_ref, block_ref = take(2)
    carried = [] if first else take(2)
    query_parts = take(len(earlier)) if last else []
    if last:
        grads, att_out = take(2)
    else:
        query_out, key_out, value_out, att_out = take(4)
    q_all, k_all, v_all, cot_all, tile_all, w_all, key_all, value_all, sems = refs

    me = lax.axis_index("seq")
    sign = 1 - 2 * lax.rem(lax.axis_index("dp"), 2)
    tokens, wide = q_all.shape[1:]
    size = wide // heads_here
    length = n * tokens
    inv_root = 1.0 / math.sqrt(size)
    place = ring_place(me, n)
    tile_of = lambda offset: ring_member(lax.rem(place + sign * offset + n, n), n)

    used = 0

    def start(copies):
        nonlocal used
        used += len(copies)
        return fetch(copies, sems, used - len(copies))

    w_copy, *tile_copies = start([(w_ref, w_all), *rows_of(tiles, tile_all)])
    block_copies = start(
        [
            (block_ref.at[:, pl.ds(i * tokens, tokens)], target)
            for i, target in enumerate((q_all, k_all, v_all))
        ]
    )
    carried_copies = start(list(zip(carried, (key_all, value_all))))
    part_copies = start(
        [
            (part.at[pl.ds(i * tokens, tokens)], grads.at[tile_of(offset), pl.ds(0, tokens)])
            for part, offsets in zip(query_parts, earlier or [])
            for i, offset in enumerate(offsets)
        ]
    )
    w_copy.wait()
    begin = 0
    for number, group in enumerate(groups):
        ids = [tile_of(offset) for offset in group]
        rows = slice(begin, begin + len(ids) * tokens)
        begin += len(ids) * tokens
        for copy in tile_copies[: len(ids)]:
            copy.wait()
        tile_copies = tile_copies[len(ids) :]
        cot_all[rows] = dot_nt(tile_all[rows], w_all[...]).astype(BF16)
        if number == 0:
            for copy in block_copies:
                copy.wait()
        for h in range(heads_here):
            cols = slice(h * size, (h + 1) * size)
            kind = (me * heads_here + h) // per_group
            bias = jnp.concatenate(
                [
                    jnp.broadcast_to(
                        jnp.concatenate(
                            [
                                jnp.full(
                                    (1, tokens),
                                    jnp.where(mask_ref[kind, t, k] == 1, 0.0, -jnp.inf),
                                    F32,
                                )
                                for k in range(n)
                            ],
                            axis=1,
                        ),
                        (tokens, length),
                    )
                    for t in ids
                ],
                axis=0,
            )
            query = jnp.concatenate([q_all[t, :, cols] for t in ids], axis=0)
            keys = k_all[:, :, cols].reshape(length, size)
            values = v_all[:, :, cols].reshape(length, size)
            cot = cot_all[rows, cols]
            scores = dot_nt(query, keys) * inv_root + bias
            expo = jnp.exp(scores - jnp.max(scores, axis=1, keepdims=True))
            probs = expo * (1.0 / jnp.sum(expo, axis=1, keepdims=True))
            probs_b = probs.astype(BF16)
            att = jnp.dot(probs_b, values, preferred_element_type=F32).astype(BF16)
            att_out[rows, cols] = att
            delta = jnp.sum(cot.astype(F32) * att.astype(F32), axis=1, keepdims=True)
            dprobs = dot_nt(cot, values)
            dscores = (probs * (dprobs - delta)).astype(BF16)
            query_grad = (jnp.dot(dscores, keys, preferred_element_type=F32) * inv_root).astype(BF16)
            key_sum = dot_tn(dscores, query)
            value_sum = dot_tn(probs_b, cot)
            if number == 0 and h == 0:
                for copy in carried_copies:
                    copy.wait()
            if number > 0 or not first:
                key_sum = key_all[:, cols] + key_sum
                value_sum = value_all[:, cols] + value_sum
            if last:
                grads[ids[0], 0:tokens, cols] = query_grad
                grads[:, tokens : 2 * tokens, cols] = (
                    (key_sum * inv_root).astype(BF16).reshape(n, tokens, size)
                )
                grads[:, 2 * tokens :, cols] = value_sum.astype(BF16).reshape(n, tokens, size)
            else:
                query_out[rows, cols] = query_grad
                if number == len(groups) - 1:
                    key_out[:, cols] = key_sum
                    value_out[:, cols] = value_sum
                else:
                    key_all[:, cols] = key_sum
                    value_all[:, cols] = value_sum
    for copy in part_copies:
        copy.wait()


def partial_kernel(part_count, tile_count, *refs):
    att_parts, tiles = refs[:part_count], refs[part_count : part_count + tile_count]
    mom_ref, out_ref, att_all, tile_all, mom_all, sems = refs[part_count + tile_count :]
    copies = fetch(
        [(mom_ref, mom_all), *rows_of(att_parts, att_all), *rows_of(tiles, tile_all)], sems
    )
    for copy in copies:
        copy.wait()
    att = att_all[...].T
    wide_d = out_ref.shape[1]
    chunk = math.gcd(wide_d, 512)
    for c in range(0, wide_d, chunk):
        cols = slice(c, c + chunk)
        grad = jnp.dot(att, tile_all[:, cols], preferred_element_type=F32)
        out_ref[:, cols] = 0.9 * mom_all[:, cols] + 0.1 * grad


def worker_kernel(heads_here, workers, part_count, tile_count, *refs):
    att_parts, tiles = refs[:part_count], refs[part_count : part_count + tile_count]
    part_ref, error_ref, *refs = refs[part_count + tile_count :]
    outs, (sent_ref, att_all, tile_all, mom_all, error_all, sems) = refs[:workers], refs[workers:]
    me = lax.axis_index("dp")
    wide, wide_d = mom_all.shape
    size = wide // heads_here
    chunk = math.gcd(wide_d, 512)
    spans = [pl.ds(h * size, size) for h in range(heads_here)]
    copies = fetch([*rows_of(att_parts, att_all), *rows_of(tiles, tile_all)], sems)
    used = len(copies)
    mom_copies = fetch([(part_ref.at[span], mom_all.at[span]) for span in spans], sems, used)
    used += heads_here
    for copy in copies:
        copy.wait()
    att = att_all[...].T
    block = size // workers
    leaving = []
    for h in range(heads_here):
        rows = slice(h * size, (h + 1) * size)
        mom_copies[h].wait()
        total = jnp.zeros((size, chunk), F32)
        for c in range(0, wide_d, chunk):
            cols = slice(c, c + chunk)
            grad = jnp.dot(att[rows], tile_all[:, cols], preferred_element_type=F32)
            mom = mom_all[rows, cols] + 0.1 * grad
            mom_all[rows, cols] = mom
            total = total + jnp.abs(mom)
        scale = jnp.sum(total, keepdims=True) * (1.0 / (size * wide_d)) + 1e-06
        inverse = 1.0 / scale
        for c in range(0, wide_d, chunk):
            cols = slice(c, c + chunk)
            mom = mom_all[rows, cols]
            sent = (scale * jnp.tanh(mom * inverse)).astype(BF16)
            sent_ref[:, cols] = sent
            error_all[rows, cols] = mom - sent.astype(F32)
        leaving += fetch([(error_all.at[spans[h]], error_ref.at[spans[h]])], sems, used + h)
        for k in range(workers):
            start = pl.multiple_of((me ^ k) * block, block)
            outs[k][h] = sent_ref[pl.ds(start, block)]
    for copy in leaving:
        copy.wait()


def server_kernel(workers, *refs):
    blocks, synced_ref, error_ref = refs[:workers], refs[workers], refs[workers + 1]
    heads_here, block, wide_d = synced_ref.shape
    for h in range(heads_here):
        total = blocks[0][h].astype(F32)
        for k in range(1, workers):
            total = total + blocks[k][h].astype(F32)
        averaged = total * (1.0 / workers)
        scale = jnp.sum(jnp.abs(averaged), keepdims=True) * (1.0 / (block * wide_d)) + 1e-06
        synced = (scale * jnp.tanh(averaged * (1.0 / scale))).astype(BF16)
        synced_ref[h] = synced
        error_ref[h] = averaged - synced.astype(F32)


def join_kernel(workers, *refs):
    blocks, out_ref = refs[:workers], refs[workers]
    me = lax.axis_index("dp")
    block = blocks[0].shape[1]
    for k in range(workers):
        start = pl.multiple_of((me ^ k) * block, block)
        out_ref[:, pl.ds(start, block), :] = blocks[k][...]


def body(qkv, tile_mask, d_out, w_out, momentum):
    n = lax.axis_size("seq")
    workers = lax.axis_size("dp")
    tokens, heads, size = qkv.shape[2:]
    heads_here = w_out.shape[0]
    groups = tile_mask.shape[0]
    per_group = heads // groups
    wide = heads_here * size
    wide_d = d_out.shape[2]
    half = n // 2
    shape = jax.ShapeDtypeStruct

    ring = ring_order(n)

    def around(turn):
        pairs = []
        for worker in range(workers):
            way = turn if worker % 2 == 0 else -turn
            pairs += [(worker * n + ring[i], worker * n + ring[(i + way) % n]) for i in range(n)]
        return lambda x: lax.ppermute(x, ("dp", "seq"), pairs)

    forward, backward = around(1), around(-1)
    own = d_out[0]
    packed_shape = (3 * tokens, wide)
    packed = pl.pallas_call(
        functools.partial(pack_kernel, n),
        out_shape=shape((n, *packed_shape), BF16),
        compiler_params=params(SMALL),
        cost_estimate=cost(0, 4 * qkv.size),
        name="pack",
    )(qkv.reshape(3 * tokens, heads, size))

    def send(blocks, k, axis):
        return lax.ppermute(blocks[k], axis, [(i, i ^ k) for i in range(len(blocks))])

    blocks = lax.all_to_all(packed, "seq", split_axis=0, concat_axis=0, tiled=True)
    w_flat = w_out.reshape(wide, wide_d)
    vmem = pl.BlockSpec(memory_space=pltpu.VMEM)
    smem = pl.BlockSpec(memory_space=pltpu.SMEM)
    anywhere = pl.BlockSpec(memory_space=pl.ANY)
    length = n * tokens

    def attend(groups, tiles, carried, earlier=None, parts=()):
        count = len(tiles)
        operands = [tile_mask, *tiles, w_flat, blocks, *carried, *parts]
        sums = shape((length, wide), F32)
        rows = shape((count * tokens, wide), BF16)
        scratch = [
            pltpu.VMEM((n, tokens, wide), BF16),
            pltpu.VMEM((n, tokens, wide), BF16),
            pltpu.VMEM((n, tokens, wide), BF16),
            pltpu.VMEM(rows.shape, BF16),
            pltpu.VMEM((count * tokens, wide_d), BF16),
            pltpu.VMEM((wide, wide_d), BF16),
            pltpu.VMEM(sums.shape, F32),
            pltpu.VMEM(sums.shape, F32),
            pltpu.SemaphoreType.DMA((count + 6 + n,)),
        ]
        if earlier is not None:
            outs = [shape((n, *packed_shape), BF16), rows]
        else:
            outs = [rows, sums, sums, rows]
        flops = count * (14 * tokens * length * wide + 2 * tokens * wide * wide_d)
        return pl.pallas_call(
            functools.partial(
                attend_kernel, n, heads_here, per_group, groups, not carried, earlier
            ),
            in_specs=[smem] + [anywhere] * (len(operands) - 1),
            out_shape=outs,
            scratch_shapes=scratch,
            compiler_params=params(LARGE),
            cost_estimate=cost(flops, count * 2**23),
            name="attend",
        )(*operands)

    fore, aft = forward(own), backward(own)
    sums, queries, listed, atts, tiles = [], [], [], [], []
    groups, fresh = [[0], [-1, 1]], [own, fore, aft]
    for s in range(1, half):
        if s < half - 1:
            next_fore, next_aft = forward(fore), backward(aft)
        else:
            far = forward(fore)
        query, *sums, att = attend(groups, fresh, sums)
        queries.append(query)
        listed.append(sum(groups, []))
        atts.append(att)
        tiles.append(fresh)
        if s == half - 2:
            joined = sum(tiles, [])
            joined_rows = len(joined) * tokens
            part = pl.pallas_call(
                functools.partial(partial_kernel, len(atts), len(joined)),
                in_specs=[anywhere] * (len(atts) + len(joined) + 1),
                out_shape=shape((wide, wide_d), F32),
                scratch_shapes=[
                    pltpu.VMEM((joined_rows, wide), BF16),
                    pltpu.VMEM((joined_rows, wide_d), BF16),
                    pltpu.VMEM((wide, wide_d), F32),
                    pltpu.SemaphoreType.DMA((len(atts) + len(joined) + 1,)),
                ],
                compiler_params=params(LARGE),
                cost_estimate=cost(2 * joined_rows * wide * wide_d, 2**24),
                name="partial",
            )(*atts, *joined, momentum.reshape(wide, wide_d))
            atts, tiles = [], []
            next_fore, next_aft, part, *sums = lax.optimization_barrier(
                [next_fore, next_aft, part, *sums]
            )
        elif s < half - 1:
            next_fore, next_aft, *sums = lax.optimization_barrier([next_fore, next_aft, *sums])
        if s < half - 1:
            fore, aft = next_fore, next_aft
            groups, fresh = [[-(s + 1), s + 1]], [fore, aft]
    grads, att = attend([[half]], [far], sums, listed, queries)
    returned = lax.all_to_all(grads, "seq", split_axis=0, concat_axis=0, tiled=True)

    atts.append(att)
    worker_tiles = [*sum(tiles, []), far]
    worker_rows = len(worker_tiles) * tokens
    error, *sent = pl.pallas_call(
        functools.partial(worker_kernel, heads_here, workers, len(atts), len(worker_tiles)),
        in_specs=[anywhere] * (len(atts) + len(worker_tiles) + 1),
        out_specs=[anywhere] + [vmem] * workers,
        out_shape=[shape((wide, wide_d), F32)]
        + [shape((heads_here, size // workers, wide_d), BF16)] * workers,
        scratch_shapes=[
            pltpu.VMEM((size, wide_d), BF16),
            pltpu.VMEM((worker_rows, wide), BF16),
            pltpu.VMEM((worker_rows, wide_d), BF16),
            pltpu.VMEM((wide, wide_d), F32),
            pltpu.VMEM((wide, wide_d), F32),
            pltpu.SemaphoreType.DMA((len(atts) + len(worker_tiles) + 2 * heads_here,)),
        ],
        compiler_params=params(LARGE),
        cost_estimate=cost(2 * worker_rows * wide * wide_d, 2**24),
        name="worker",
    )(*atts, *worker_tiles, part)
    received = [sent[0]] + [send(sent, k, "dp") for k in range(1, workers)]

    synced, server_error = pl.pallas_call(
        functools.partial(server_kernel, workers),
        out_shape=[
            shape((heads_here, size // workers, wide_d), BF16),
            shape((heads_here, size // workers, wide_d), F32),
        ],
        compiler_params=params(SMALL),
        cost_estimate=cost(0, 2**22),
        name="server",
    )(*received)
    gathered = [synced] + [None] * (workers - 1)
    for k in range(1, workers):
        source, step = (synced, k) if k == 1 or k % 2 == 0 else (gathered[k - 1], 1)
        gathered[k] = lax.ppermute(source, "dp", [(i, i ^ step) for i in range(workers)])

    grad_rows = pl.pallas_call(
        functools.partial(unpack_kernel, n),
        out_shape=shape((3 * tokens, heads, size), BF16),
        compiler_params=params(SMALL),
        cost_estimate=cost(0, 4 * qkv.size),
        name="unpack",
    )(returned)
    synced_momentum = pl.pallas_call(
        functools.partial(join_kernel, workers),
        out_shape=shape((heads_here, size, wide_d), BF16),
        compiler_params=params(SMALL),
        cost_estimate=cost(0, 4 * w_out.size),
        name="join",
    )(*gathered)
    return (
        grad_rows.reshape(qkv.shape),
        synced_momentum,
        error.reshape(1, heads_here, size, wide_d),
        server_error,
    )


def solution(mesh):
    placed = (
        P(None, "dp", "seq", None, None),
        P(),
        P("dp", "seq", None),
        P("seq", None, None),
        P("seq", None, None),
    )
    return jax.shard_map(
        body,
        mesh=mesh,
        in_specs=placed,
        out_specs=(
            P(None, "dp", "seq", None, None),
            P("seq", None, None),
            P("dp", "seq", None, None),
            P("seq", "dp", None),
        ),
        check_vma=False,
    )
```

```python
import functools
import math

import jax
import jax.numpy as jnp
from jax import lax
from jax.experimental import pallas as pl
from jax.experimental.pallas import tpu as pltpu
from jax.sharding import PartitionSpec as P

SMALL, LARGE = 16 * 1024 * 1024, 60 * 1024 * 1024
F32 = jnp.float32
BF16 = jnp.bfloat16


def params(limit):
    return pltpu.CompilerParams(vmem_limit_bytes=limit)


def cost(flops, moved):
    return pl.CostEstimate(flops=flops, bytes_accessed=moved, transcendentals=0)


def ring_order(n):
    return [i for i in range(n) if i % 2 == 0] + [i for i in reversed(range(n)) if i % 2]


def ring_member(place, n):
    return jnp.where(place < n // 2, 2 * place, 2 * n - 1 - 2 * place)


def ring_place(member, n):
    return jnp.where(member % 2 == 0, member // 2, (2 * n - 1 - member) // 2)


def waves_of(n):
    odd, even = list(range(n - 1, 1, -2)), list(range(n - 2, 0, -2))
    return [[1, *odd], even]


def dot_nt(a, b):
    return lax.dot_general(a, b, (((1,), (1,)), ((), ())), preferred_element_type=F32)


def dot_tn(a, b):
    return lax.dot_general(a, b, (((0,), (0,)), ((), ())), preferred_element_type=F32)


def pack_kernel(n, x_ref, *refs):
    outs, parts = refs[:n], refs[n]
    rows, heads, size = x_ref.shape
    wide = heads * size // n
    x = x_ref[...].reshape(rows, heads * size)
    for d in range(n):
        parts[d] = x[:, d * wide : (d + 1) * wide]
    me = lax.axis_index("seq")
    for k in range(n):
        outs[k][...] = parts[me ^ k]


def unpack_kernel(n, blocks, out_ref):
    out_ref[...] = jnp.concatenate([blocks[d] for d in range(n)], axis=1).reshape(out_ref.shape)


def fetch(copies, sems, first=0):
    started = [
        pltpu.make_async_copy(source, target, sems.at[first + i])
        for i, (source, target) in enumerate(copies)
    ]
    for copy in started:
        copy.start()
    return started


def rows_of(tiles, buffer):
    copies, start = [], 0
    for tile in tiles:
        copies.append((tile, buffer.at[pl.ds(start, tile.shape[0])]))
        start += tile.shape[0]
    return copies


def attend_kernel(n, heads_here, per_group, groups, first, earlier, far, mask_ref, *refs):
    refs = list(refs)
    count = sum(len(g) for g in groups)
    take = lambda m: [refs.pop(0) for _ in range(m)]
    tiles = take(count)
    (w_ref,) = take(1)
    blocks = take(n)
    carried = [] if first else take(2)
    (mom_ref,) = take(1) if first else [None]
    query_parts = [] if earlier is None else take(len(earlier))
    if far:
        far_probs_ref, far_att_ref, query_ref, grads = take(4)
    else:
        query_out, key_out, value_out, att_out = take(4)
    if first:
        far_probs_out, far_att_out, part_out = take(3)
    q_all, k_all, v_all, cot_all, tile_all, w_all, key_all, value_all, sems = take(9)
    if far:
        far_probs, far_att = take(2)
    if first:
        (mom_all,) = take(1)

    me = lax.axis_index("seq")
    sign = 1 - 2 * lax.rem(lax.axis_index("dp"), 2)
    tokens, wide = q_all.shape[1:]
    size = wide // heads_here
    length = n * tokens
    inv_root = 1.0 / math.sqrt(size)
    place = ring_place(me, n)
    tile_of = lambda offset: ring_member(lax.rem(place + sign * offset + n, n), n)

    used = 0

    def start(copies):
        nonlocal used
        used += len(copies)
        return fetch(copies, sems, used - len(copies))

    w_copy, *tile_copies = start([(w_ref, w_all), *rows_of(tiles, tile_all)])
    block_copies = start(
        [
            (block.at[pl.ds(i * tokens, tokens)], target.at[me ^ k])
            for k, block in enumerate(blocks)
            for i, target in enumerate((q_all, k_all, v_all))
        ]
    )
    carried_copies = start(list(zip(carried, (key_all, value_all))))
    mom_copies = start([(mom_ref, mom_all)] if first else [])
    far_copies = start([(far_probs_ref, far_probs), (far_att_ref, far_att)] if far else [])
    if far:
        part_copies = start([(query_ref, grads.at[:, pl.ds(0, tokens)])])
    else:
        part_copies = start(
            [
                (part.at[pl.ds(i * tokens, tokens)], query_out.at[tile_of(offset)])
                for part, offsets in zip(query_parts, earlier or [])
                for i, offset in enumerate(offsets)
            ]
        )
    if earlier is not None:
        query_out[tile_of(n // 2)] = jnp.zeros((tokens, wide), BF16)

    def forward(ids, h):
        cols = slice(h * size, (h + 1) * size)
        kind = (me * heads_here + h) // per_group
        bias = [
            jnp.concatenate(
                [
                    jnp.full(
                        (1, tokens), jnp.where(mask_ref[kind, t, k] == 1, 0.0, -jnp.inf), F32
                    )
                    for k in range(n)
                ],
                axis=1,
            )
            for t in ids
        ]
        bias = jnp.concatenate([jnp.broadcast_to(b, (tokens, length)) for b in bias], axis=0)
        query = jnp.concatenate([q_all[t, :, cols] for t in ids], axis=0)
        keys = k_all[:, :, cols].reshape(length, size)
        values = v_all[:, :, cols].reshape(length, size)
        scores = dot_nt(query, keys) * inv_root + bias
        expo = jnp.exp(scores - jnp.max(scores, axis=1, keepdims=True))
        probs = expo * (1.0 / jnp.sum(expo, axis=1, keepdims=True))
        att = jnp.dot(probs.astype(BF16), values, preferred_element_type=F32).astype(BF16)
        return probs, att

    w_copy.wait()
    begin = 0
    for number, group in enumerate(groups):
        ids = [tile_of(offset) for offset in group]
        rows = slice(begin, begin + len(ids) * tokens)
        begin += len(ids) * tokens
        for copy in tile_copies[: len(ids)]:
            copy.wait()
        tile_copies = tile_copies[len(ids) :]
        cot_all[rows] = dot_nt(tile_all[rows], w_all[...]).astype(BF16)
        if number == 0:
            for copy in block_copies + far_copies:
                copy.wait()
        for h in range(heads_here):
            cols = slice(h * size, (h + 1) * size)
            if far:
                probs, att = far_probs[h], far_att[:, cols]
            else:
                probs, att = forward(ids, h)
                att_out[rows, cols] = att
            probs_b = probs.astype(BF16)
            query = jnp.concatenate([q_all[t, :, cols] for t in ids], axis=0)
            keys = k_all[:, :, cols].reshape(length, size)
            values = v_all[:, :, cols].reshape(length, size)
            cot = cot_all[rows, cols]
            delta = jnp.sum(cot.astype(F32) * att.astype(F32), axis=1, keepdims=True)
            dprobs = dot_nt(cot, values)
            dscores = (probs * (dprobs - delta)).astype(BF16)
            query_grad = (jnp.dot(dscores, keys, preferred_element_type=F32) * inv_root).astype(BF16)
            if far:
                if h == 0:
                    part_copies.pop().wait()
                grads[ids[0], 0:tokens, cols] = query_grad
            elif earlier is None:
                query_out[rows, cols] = query_grad
            else:
                for i, t in enumerate(ids):
                    query_out[t, :, cols] = query_grad[i * tokens : (i + 1) * tokens]
            key_sum = dot_tn(dscores, query)
            value_sum = dot_tn(probs_b, cot)
            if number == 0 and h == 0:
                for copy in carried_copies:
                    copy.wait()
            if number > 0 or not first:
                key_sum = key_all[:, cols] + key_sum
                value_sum = value_all[:, cols] + value_sum
            if far:
                grads[:, tokens : 2 * tokens, cols] = (
                    (key_sum * inv_root).astype(BF16).reshape(n, tokens, size)
                )
                grads[:, 2 * tokens :, cols] = value_sum.astype(BF16).reshape(n, tokens, size)
            elif number == len(groups) - 1:
                key_out[:, cols] = key_sum
                value_out[:, cols] = value_sum
            else:
                key_all[:, cols] = key_sum
                value_all[:, cols] = value_sum
    if first:
        for h in range(heads_here):
            probs, att = forward([tile_of(n // 2)], h)
            far_probs_out[h] = probs
            far_att_out[:, h * size : (h + 1) * size] = att
        for copy in mom_copies:
            copy.wait()
        wide_d = mom_all.shape[1]
        chunk = math.gcd(wide_d, 512)
        att = att_out[...].T
        leaving = []
        for c in range(0, wide_d, chunk):
            cols = slice(c, c + chunk)
            grad = jnp.dot(att, tile_all[:, cols], preferred_element_type=F32)
            mom_all[:, cols] = 0.9 * mom_all[:, cols] + 0.1 * grad
            span = pl.ds(c, chunk)
            leaving += start([(mom_all.at[:, span], part_out.at[:, span])])
        for copy in leaving:
            copy.wait()
    for copy in part_copies:
        copy.wait()


def worker_kernel(heads_here, workers, part_count, tile_count, *refs):
    att_parts, tiles = refs[:part_count], refs[part_count : part_count + tile_count]
    part_ref, error_ref, *refs = refs[part_count + tile_count :]
    outs, (sent_ref, att_all, tile_all, mom_all, error_all, sems) = refs[:workers], refs[workers:]
    me = lax.axis_index("dp")
    wide, wide_d = mom_all.shape
    size = wide // heads_here
    chunk = math.gcd(wide_d, 512)
    used = part_count + tile_count + heads_here
    spans = [pl.ds(h * size, size) for h in range(heads_here)]
    copies = fetch([*rows_of(att_parts, att_all), *rows_of(tiles, tile_all)], sems)
    mom_copies = fetch([(part_ref.at[s], mom_all.at[s]) for s in spans], sems, len(copies))
    for copy in copies:
        copy.wait()
    att = att_all[...].T
    block = size // workers
    leaving = []
    for h in range(heads_here):
        rows = slice(h * size, (h + 1) * size)
        mom_copies[h].wait()
        total = jnp.zeros((size, chunk), F32)
        for c in range(0, wide_d, chunk):
            cols = slice(c, c + chunk)
            grad = jnp.dot(att[rows], tile_all[:, cols], preferred_element_type=F32)
            mom = mom_all[rows, cols] + 0.1 * grad
            mom_all[rows, cols] = mom
            total = total + jnp.abs(mom)
        scale = jnp.sum(total, keepdims=True) * (1.0 / (size * wide_d)) + 1e-06
        inverse = 1.0 / scale
        for c in range(0, wide_d, chunk):
            cols = slice(c, c + chunk)
            mom = mom_all[rows, cols]
            sent = (scale * jnp.tanh(mom * inverse)).astype(BF16)
            sent_ref[h, :, cols] = sent
            error_all[rows, cols] = mom - sent.astype(F32)
        going = [(error_all.at[spans[h]], error_ref.at[spans[h]])]
        for k in range(workers):
            start = pl.multiple_of((me ^ k) * block, block)
            going.append((sent_ref.at[h, pl.ds(start, block)], outs[k].at[h]))
        leaving += fetch(going, sems, used + h * len(going))
    for copy in leaving:
        copy.wait()


def server_kernel(workers, *refs):
    blocks, synced_ref, error_ref = refs[:workers], refs[workers], refs[workers + 1]
    heads_here, block, wide_d = synced_ref.shape
    for h in range(heads_here):
        total = blocks[0][h].astype(F32)
        for k in range(1, workers):
            total = total + blocks[k][h].astype(F32)
        averaged = total * (1.0 / workers)
        scale = jnp.sum(jnp.abs(averaged), keepdims=True) * (1.0 / (block * wide_d)) + 1e-06
        synced = (scale * jnp.tanh(averaged * (1.0 / scale))).astype(BF16)
        synced_ref[h] = synced
        error_ref[h] = averaged - synced.astype(F32)


def join_kernel(workers, *refs):
    blocks, out_ref = refs[:workers], refs[workers]
    me = lax.axis_index("dp")
    block = blocks[0].shape[1]
    for k in range(workers):
        start = pl.multiple_of((me ^ k) * block, block)
        out_ref[:, pl.ds(start, block), :] = blocks[k][...]


def body(qkv, tile_mask, d_out, w_out, momentum):
    n = lax.axis_size("seq")
    workers = lax.axis_size("dp")
    tokens, heads, size = qkv.shape[2:]
    heads_here = w_out.shape[0]
    groups = tile_mask.shape[0]
    per_group = heads // groups
    wide = heads_here * size
    wide_d = d_out.shape[2]
    half = n // 2
    shape = jax.ShapeDtypeStruct

    ring = ring_order(n)

    def around(turn):
        pairs = []
        for worker in range(workers):
            way = turn if worker % 2 == 0 else -turn
            pairs += [(worker * n + ring[i], worker * n + ring[(i + way) % n]) for i in range(n)]
        return lambda x: lax.ppermute(x, ("dp", "seq"), pairs)

    forward, backward = around(1), around(-1)
    own = d_out[0]
    packed_shape = (3 * tokens, wide)
    packed = pl.pallas_call(
        functools.partial(pack_kernel, n),
        out_shape=[shape(packed_shape, BF16)] * n,
        scratch_shapes=[pltpu.VMEM((n, *packed_shape), BF16)],
        compiler_params=params(SMALL),
        cost_estimate=cost(0, 4 * qkv.size),
        name="pack",
    )(qkv.reshape(3 * tokens, heads, size))

    def send(blocks, k, axis):
        return lax.ppermute(blocks[k], axis, [(i, i ^ k) for i in range(len(blocks))])

    blocks = list(packed)
    w_flat = w_out.reshape(wide, wide_d)
    vmem = pl.BlockSpec(memory_space=pltpu.VMEM)
    smem = pl.BlockSpec(memory_space=pltpu.SMEM)
    anywhere = pl.BlockSpec(memory_space=pl.ANY)
    length = n * tokens

    def attend(groups, tiles, carried, earlier=None, parts=(), far=()):
        count = len(tiles)
        carried = carried or [momentum.reshape(wide, wide_d)]
        first = len(carried) == 1
        operands = [tile_mask, *tiles, w_flat, *blocks, *carried, *parts, *far]
        sums = shape((length, wide), F32)
        rows = shape((count * tokens, wide), BF16)
        probs = shape((heads_here, tokens, length), F32)
        scratch = [
            pltpu.VMEM((n, tokens, wide), BF16),
            pltpu.VMEM((n, tokens, wide), BF16),
            pltpu.VMEM((n, tokens, wide), BF16),
            pltpu.VMEM(rows.shape, BF16),
            pltpu.VMEM((count * tokens, wide_d), BF16),
            pltpu.VMEM((wide, wide_d), BF16),
            pltpu.VMEM(sums.shape, F32),
            pltpu.VMEM(sums.shape, F32),
            pltpu.SemaphoreType.DMA((count + 8 + 4 * n + wide_d // math.gcd(wide_d, 512),)),
        ]
        if far:
            outs = [shape((n, *packed_shape), BF16)]
            scratch += [pltpu.VMEM(probs.shape, F32), pltpu.VMEM((tokens, wide), BF16)]
        else:
            outs = [rows, sums, sums, rows]
        if earlier is not None:
            outs[0] = shape((n, tokens, wide), BF16)
        out_specs = [vmem] * len(outs)
        if first:
            outs += [probs, shape((tokens, wide), BF16), shape((wide, wide_d), F32)]
            out_specs += [vmem, vmem, anywhere]
            scratch += [pltpu.VMEM((wide, wide_d), F32)]
        flops = count * (14 * tokens * length * wide + 2 * tokens * wide * wide_d)
        if len(outs) == 1:
            outs, out_specs = outs[0], vmem
        return pl.pallas_call(
            functools.partial(
                attend_kernel, n, heads_here, per_group, groups, first, earlier, bool(far)
            ),
            in_specs=[smem] + [anywhere] * (len(operands) - 1),
            out_specs=out_specs,
            out_shape=outs,
            scratch_shapes=scratch,
            compiler_params=params(LARGE),
            cost_estimate=cost(flops, count * 2**23),
            name="attend",
        )(*operands)

    waves = waves_of(n)
    early = [[0]] + [[-s, s] for s in range(1, len(waves) + 1)]
    early_tiles, fore, aft = [own], own, own
    for wave in waves:
        fore, aft, *got = lax.optimization_barrier(
            [forward(fore), backward(aft), *[send(packed, k, "seq") for k in wave]]
        )
        early_tiles += [fore, aft]
        for k, block in zip(wave, got):
            blocks[k] = block

    groups, fresh, sums, queries, listed, atts, tiles = early, early_tiles, [], [], [], [], []
    for s in range(len(waves), half):
        if s < half - 1:
            next_fore, next_aft = forward(fore), backward(aft)
            gather = ()
        else:
            far = forward(fore)
            gather = (listed, queries)
        query, key_sum, value_sum, att, *saved = attend(groups, fresh, sums, *gather)
        sums = [key_sum, value_sum]
        if saved:
            far_probs, far_att, part = saved
        else:
            atts.append(att)
            tiles += fresh
        if s < half - 1:
            fore, aft, query, *sums = lax.optimization_barrier(
                [next_fore, next_aft, query, *sums]
            )
            listed.append(sum(groups, []))
            queries.append(query)
            groups, fresh = [[-(s + 1), s + 1]], [fore, aft]
    grads = attend([[half]], [far], sums, far=(far_probs, far_att, query))
    returned = lax.all_to_all(grads, "seq", split_axis=0, concat_axis=0, tiled=True)

    atts.append(far_att)
    worker_tiles = [*tiles, far]
    worker_rows = len(worker_tiles) * tokens
    worker_copies = len(atts) + len(worker_tiles) + heads_here * (workers + 2)
    error, *sent = pl.pallas_call(
        functools.partial(worker_kernel, heads_here, workers, len(atts), len(worker_tiles)),
        in_specs=[anywhere] * (len(atts) + len(worker_tiles) + 1),
        out_specs=[anywhere] * (1 + workers),
        out_shape=[shape((wide, wide_d), F32)]
        + [shape((heads_here, size // workers, wide_d), BF16)] * workers,
        scratch_shapes=[
            pltpu.VMEM((heads_here, size, wide_d), BF16),
            pltpu.VMEM((worker_rows, wide), BF16),
            pltpu.VMEM((worker_rows, wide_d), BF16),
            pltpu.VMEM((wide, wide_d), F32),
            pltpu.VMEM((wide, wide_d), F32),
            pltpu.SemaphoreType.DMA((worker_copies,)),
        ],
        compiler_params=params(LARGE),
        cost_estimate=cost(2 * worker_rows * wide * wide_d, 2**24),
        name="worker",
    )(*atts, *worker_tiles, part)
    received = [sent[0]] + [send(sent, k, "dp") for k in range(1, workers)]

    synced, server_error = pl.pallas_call(
        functools.partial(server_kernel, workers),
        out_shape=[
            shape((heads_here, size // workers, wide_d), BF16),
            shape((heads_here, size // workers, wide_d), F32),
        ],
        compiler_params=params(SMALL),
        cost_estimate=cost(0, 2**22),
        name="server",
    )(*received)
    gathered = [synced] + [None] * (workers - 1)
    for k in range(1, workers):
        source, step = (synced, k) if k == 1 or k % 2 == 0 else (gathered[k - 1], 1)
        gathered[k] = lax.ppermute(source, "dp", [(i, i ^ step) for i in range(workers)])

    grad_rows = pl.pallas_call(
        functools.partial(unpack_kernel, n),
        out_shape=shape((3 * tokens, heads, size), BF16),
        compiler_params=params(SMALL),
        cost_estimate=cost(0, 4 * qkv.size),
        name="unpack",
    )(returned)
    synced_momentum = pl.pallas_call(
        functools.partial(join_kernel, workers),
        out_shape=shape((heads_here, size, wide_d), BF16),
        compiler_params=params(SMALL),
        cost_estimate=cost(0, 4 * w_out.size),
        name="join",
    )(*gathered)
    return (
        grad_rows.reshape(qkv.shape),
        synced_momentum,
        error.reshape(1, heads_here, size, wide_d),
        server_error,
    )


def solution(mesh):
    placed = (
        P(None, "dp", "seq", None, None),
        P(),
        P("dp", "seq", None),
        P("seq", None, None),
        P("seq", None, None),
    )
    return jax.shard_map(
        body,
        mesh=mesh,
        in_specs=placed,
        out_specs=(
            P(None, "dp", "seq", None, None),
            P("seq", None, None),
            P("dp", "seq", None, None),
            P("seq", "dp", None),
        ),
        check_vma=False,
    )
```

```python
import functools
import math

import jax
import jax.numpy as jnp
from jax import lax
from jax.experimental import pallas as pl
from jax.experimental.pallas import tpu as pltpu
from jax.sharding import PartitionSpec as P

SMALL, LARGE = 16 * 1024 * 1024, 63 * 1024 * 1024
F32 = jnp.float32
HEAVY = 10**13, 10**13, 10**13
BF16 = jnp.bfloat16


def params(limit):
    return pltpu.CompilerParams(vmem_limit_bytes=limit)


def cost(flops, moved):
    return pl.CostEstimate(flops=flops, bytes_accessed=moved, transcendentals=0)


def ring_order(n):
    return [i for i in range(n) if i % 2 == 0] + [i for i in reversed(range(n)) if i % 2]


def ring_member(place, n):
    return jnp.where(place < n // 2, 2 * place, 2 * n - 1 - 2 * place)


def ring_place(member, n):
    return jnp.where(member % 2 == 0, member // 2, (2 * n - 1 - member) // 2)


def waves_of(n):
    odd, even = list(range(n - 1, 1, -2)), list(range(n - 2, 0, -2))
    return [[1, *odd], even]


def dot_nt(a, b):
    return lax.dot_general(a, b, (((1,), (1,)), ((), ())), preferred_element_type=F32)


def dot_tn(a, b):
    return lax.dot_general(a, b, (((0,), (0,)), ((), ())), preferred_element_type=F32)


def pack_kernel(n, x_ref, *refs):
    outs, parts = refs[:n], refs[n]
    rows, heads, size = x_ref.shape
    wide = heads * size // n
    x = x_ref[...].reshape(rows, heads * size)
    for d in range(n):
        parts[d] = x[:, d * wide : (d + 1) * wide]
    me = lax.axis_index("seq")
    for k in range(n):
        outs[k][...] = parts[me ^ k]


def unpack_kernel(n, queries_ref, far_ref, others_ref, out_ref, blocks, far_all, rows, sems):
    tokens = far_ref.shape[0]
    me = lax.axis_index("seq")
    spans = [pl.ds(i * tokens, tokens) for i in range(3)]
    copies = fetch(
        [(queries_ref, blocks.at[:, spans[0]]), (far_ref, far_all)]
        + [(others_ref.at[:, spans[i]], blocks.at[:, spans[i + 1]]) for i in range(2)],
        sems,
    )
    copies.pop(0).wait()
    leaving = []
    for i, copy in enumerate(copies):
        copy.wait()
        here = slice(i * tokens, (i + 1) * tokens)
        if i == 0:
            far_place = ring_member(lax.rem(ring_place(me, n) + n // 2, n), n)
            blocks[far_place, here] = far_all[...]
        joined = jnp.concatenate([blocks[d, here] for d in range(n)], axis=1)
        rows[here] = joined.reshape(tokens, *rows.shape[1:])
        leaving += fetch([(rows.at[spans[i]], out_ref.at[spans[i]])], sems, 4 + i)
    for copy in leaving:
        copy.wait()


def fetch(copies, sems, first=0):
    started = [
        pltpu.make_async_copy(source, target, sems.at[first + i])
        for i, (source, target) in enumerate(copies)
    ]
    for copy in started:
        copy.start()
    return started


def rows_of(tiles, buffer):
    copies, start = [], 0
    for tile in tiles:
        copies.append((tile, buffer.at[pl.ds(start, tile.shape[0])]))
        start += tile.shape[0]
    return copies


def attend_kernel(n, heads_here, per_group, groups, first, earlier, far, mask_ref, *refs, beside=None):
    refs = list(refs)
    count = sum(len(g) for g in groups)
    take = lambda m: [refs.pop(0) for _ in range(m)]
    tiles = take(count)
    (w_ref,) = take(1)
    blocks = take(n)
    carried = [] if first else take(2)
    (mom_ref,) = take(1) if first else [None]
    query_parts = [] if earlier is None else take(len(earlier))
    if far:
        far_probs_ref, far_att_ref, query_out, grads_out = take(4)
    else:
        query_out, key_out, value_out, att_out = take(4)
    if first:
        far_probs_out, far_att_out, part_out = take(3)
    qkv_all, cot_all, tile_all, w_all, key_all, value_all, sems = take(7)
    if far:
        far_probs, far_att, grads = take(3)
    if first:
        (mom_all,) = take(1)

    me = lax.axis_index("seq")
    sign = 1 - 2 * lax.rem(lax.axis_index("dp"), 2)
    wide = qkv_all.shape[2]
    tokens = qkv_all.shape[1] // 3
    size = wide // heads_here
    length = n * tokens
    queries_of = lambda ids, cols: jnp.concatenate([qkv_all[t, 0:tokens, cols] for t in ids], axis=0)
    keys_of = lambda cols: qkv_all[:, tokens : 2 * tokens, cols].reshape(length, size)
    values_of = lambda cols: qkv_all[:, 2 * tokens :, cols].reshape(length, size)
    inv_root = 1.0 / math.sqrt(size)
    place = ring_place(me, n)
    tile_of = lambda offset: ring_member(lax.rem(place + sign * offset + n, n), n)

    used = 0

    def start(copies):
        nonlocal used
        used += len(copies)
        return fetch(copies, sems, used - len(copies))

    w_copy, *tile_copies = start([(w_ref, w_all), *rows_of(tiles, tile_all)])
    att_copies = start([(far_att_ref, far_att)] if far else [])
    work = beside(tile_all, far_att) if beside else None
    far_copies = start([(far_probs_ref, far_probs)] if far else [])
    block_copies = start([(block, qkv_all.at[me ^ k]) for k, block in enumerate(blocks)])
    carried_copies = start(list(zip(carried, (key_all, value_all))))
    mom_copies = start([(mom_ref, mom_all)] if first else [])
    part_copies = start(
        [
            (part.at[pl.ds(i * tokens, tokens)], query_out.at[tile_of(offset)])
            for part, offsets in zip(query_parts, earlier or [])
            for i, offset in enumerate(offsets)
        ]
    )
    leaving = []
    if earlier is not None:
        query_out[tile_of(n // 2)] = jnp.zeros((tokens, wide), BF16)

    def forward(ids, h):
        cols = slice(h * size, (h + 1) * size)
        kind = (me * heads_here + h) // per_group
        bias = [
            jnp.concatenate(
                [
                    jnp.full(
                        (1, tokens), jnp.where(mask_ref[kind, t, k] == 1, 0.0, -jnp.inf), F32
                    )
                    for k in range(n)
                ],
                axis=1,
            )
            for t in ids
        ]
        bias = jnp.concatenate([jnp.broadcast_to(b, (tokens, length)) for b in bias], axis=0)
        scores = dot_nt(queries_of(ids, cols), keys_of(cols)) * inv_root + bias
        expo = jnp.exp(scores - jnp.max(scores, axis=1, keepdims=True))
        probs = expo * (1.0 / jnp.sum(expo, axis=1, keepdims=True))
        att = jnp.dot(probs.astype(BF16), values_of(cols), preferred_element_type=F32).astype(BF16)
        return probs, att

    w_copy.wait()
    begin = 0
    for number, group in enumerate(groups):
        ids = [tile_of(offset) for offset in group]
        rows = slice(begin, begin + len(ids) * tokens)
        begin += len(ids) * tokens
        for copy in tile_copies[: len(ids)]:
            copy.wait()
        tile_copies = tile_copies[len(ids) :]
        cot_all[rows] = dot_nt(tile_all[rows], w_all[...]).astype(BF16)
        if work:
            att_copies.pop().wait()
            leaving += work()
        if number == 0:
            for copy in block_copies + far_copies:
                copy.wait()
        for h in range(heads_here):
            cols = slice(h * size, (h + 1) * size)
            if far:
                probs, att = far_probs[h], far_att[:, cols]
            else:
                probs, att = forward(ids, h)
                att_out[rows, cols] = att
            probs_b = probs.astype(BF16)
            cot = cot_all[rows, cols]
            delta = jnp.sum(cot.astype(F32) * att.astype(F32), axis=1, keepdims=True)
            dprobs = dot_nt(cot, values_of(cols))
            dscores = (probs * (dprobs - delta)).astype(BF16)
            query_grad = jnp.dot(dscores, keys_of(cols), preferred_element_type=F32) * inv_root
            query_grad = query_grad.astype(BF16)
            if earlier is None:
                query_out[rows, cols] = query_grad
            else:
                for i, t in enumerate(ids):
                    query_out[t, :, cols] = query_grad[i * tokens : (i + 1) * tokens]
            key_sum = dot_tn(dscores, queries_of(ids, cols))
            value_sum = dot_tn(probs_b, cot)
            if number == 0 and h == 0:
                for copy in carried_copies:
                    copy.wait()
            if number > 0 or not first:
                key_sum = key_all[:, cols] + key_sum
                value_sum = value_all[:, cols] + value_sum
            if far:
                grads[:, 0:tokens, cols] = (
                    (key_sum * inv_root).astype(BF16).reshape(n, tokens, size)
                )
                grads[:, tokens:, cols] = value_sum.astype(BF16).reshape(n, tokens, size)
                span = pl.ds(h * size, size)
                leaving += start([(grads.at[:, :, span], grads_out.at[:, :, span])])
            elif number == len(groups) - 1:
                key_out[:, cols] = key_sum
                value_out[:, cols] = value_sum
            else:
                key_all[:, cols] = key_sum
                value_all[:, cols] = value_sum
    if first:
        for h in range(heads_here):
            probs, att = forward([tile_of(n // 2)], h)
            far_probs_out[h] = probs
            far_att_out[:, h * size : (h + 1) * size] = att
        for copy in mom_copies:
            copy.wait()
        wide_d = mom_all.shape[1]
        chunk = math.gcd(wide_d, 512)
        att = att_out[...].T
        for c in range(0, wide_d, chunk):
            cols = slice(c, c + chunk)
            grad = jnp.dot(att, tile_all[:, cols], preferred_element_type=F32)
            mom_all[:, cols] = 0.9 * mom_all[:, cols] + 0.1 * grad
            span = pl.ds(c, chunk)
            leaving += start([(mom_all.at[:, span], part_out.at[:, span])])
    for copy in part_copies + leaving:
        copy.wait()


def tail_kernel(n, heads_here, per_group, workers, tile_count, *refs):
    refs = list(refs)
    take = lambda m: [refs.pop(0) for _ in range(m)]
    attend_in = take(1 + 2 + n + 2 + 2)
    att_parts, tiles, (part_ref,) = take(tile_count // 2), take(tile_count), take(1)
    attend_out, (error_ref,), outs = take(2), take(1), take(workers)
    sent_ref, att_all, more_tiles, mom_all, error_all, worker_sems, *attend_scratch = refs

    def beside(far_tile, far_att):
        wide, wide_d = mom_all.shape
        size = wide // heads_here
        chunk = math.gcd(wide_d, 512)
        block = size // workers
        spans = [pl.ds(h * size, size) for h in range(heads_here)]
        copies = [*rows_of(att_parts, att_all), *rows_of(tiles, more_tiles)]
        copies = fetch(copies, worker_sems)
        mom_copies = fetch(
            [(part_ref.at[s], mom_all.at[s]) for s in spans], worker_sems, len(copies)
        )
        used = len(copies) + heads_here

        def work():
            for copy in copies:
                copy.wait()
            att, late = att_all[...].T, far_att[...].T
            leaving = []
            for h in range(heads_here):
                rows = slice(h * size, (h + 1) * size)
                mom_copies[h].wait()
                total = jnp.zeros((size, chunk), F32)
                for c in range(0, wide_d, chunk):
                    cols = slice(c, c + chunk)
                    grad = jnp.dot(att[rows], more_tiles[:, cols], preferred_element_type=F32)
                    grad += jnp.dot(late[rows], far_tile[:, cols], preferred_element_type=F32)
                    mom = mom_all[rows, cols] + 0.1 * grad
                    mom_all[rows, cols] = mom
                    total = total + jnp.abs(mom)
                scale = jnp.sum(total, keepdims=True) * (1.0 / (size * wide_d)) + 1e-06
                inverse = 1.0 / scale
                for c in range(0, wide_d, chunk):
                    cols = slice(c, c + chunk)
                    mom = mom_all[rows, cols]
                    sent = (scale * jnp.tanh(mom * inverse)).astype(BF16)
                    sent_ref[h, :, cols] = sent
                    error_all[rows, cols] = mom - sent.astype(F32)
                me = lax.axis_index("dp")
                going = [(error_all.at[spans[h]], error_ref.at[spans[h]])]
                for k in range(workers):
                    start = pl.multiple_of((me ^ k) * block, block)
                    going.append((sent_ref.at[h, pl.ds(start, block)], outs[k].at[h]))
                leaving.extend(fetch(going, worker_sems, used + h * len(going)))
            return leaving

        return work

    attend_kernel(
        n, heads_here, per_group, [[n // 2]], False, None, True,
        *attend_in, *attend_out, *attend_scratch, beside=beside,
    )


def server_kernel(workers, *refs):
    blocks, synced_ref, error_ref = refs[:workers], refs[workers], refs[workers + 1]
    heads_here, block, wide_d = synced_ref.shape
    for h in range(heads_here):
        total = blocks[0][h].astype(F32)
        for k in range(1, workers):
            total = total + blocks[k][h].astype(F32)
        averaged = total * (1.0 / workers)
        scale = jnp.sum(jnp.abs(averaged), keepdims=True) * (1.0 / (block * wide_d)) + 1e-06
        synced = (scale * jnp.tanh(averaged * (1.0 / scale))).astype(BF16)
        synced_ref[h] = synced
        error_ref[h] = averaged - synced.astype(F32)


def join_kernel(workers, *refs):
    blocks, out_ref = refs[:workers], refs[workers]
    me = lax.axis_index("dp")
    block = blocks[0].shape[1]
    for k in range(workers):
        start = pl.multiple_of((me ^ k) * block, block)
        out_ref[:, pl.ds(start, block), :] = blocks[k][...]


def body(qkv, tile_mask, d_out, w_out, momentum):
    n = lax.axis_size("seq")
    workers = lax.axis_size("dp")
    tokens, heads, size = qkv.shape[2:]
    heads_here = w_out.shape[0]
    groups = tile_mask.shape[0]
    per_group = heads // groups
    wide = heads_here * size
    wide_d = d_out.shape[2]
    half = n // 2
    shape = jax.ShapeDtypeStruct

    ring = ring_order(n)

    def around(turn):
        pairs = []
        for worker in range(workers):
            way = turn if worker % 2 == 0 else -turn
            pairs += [(worker * n + ring[i], worker * n + ring[(i + way) % n]) for i in range(n)]
        return lambda x: lax.ppermute(x, ("dp", "seq"), pairs)

    forward, backward = around(1), around(-1)
    own = d_out[0]
    packed_shape = (3 * tokens, wide)
    packed = pl.pallas_call(
        functools.partial(pack_kernel, n),
        out_shape=[shape(packed_shape, BF16)] * n,
        scratch_shapes=[pltpu.VMEM((n, *packed_shape), BF16)],
        compiler_params=params(SMALL),
        cost_estimate=cost(0, 4 * qkv.size),
        name="pack",
    )(qkv.reshape(3 * tokens, heads, size))

    def send(blocks, k, axis):
        return lax.ppermute(blocks[k], axis, [(i, i ^ k) for i in range(len(blocks))])

    blocks = list(packed)
    w_flat = w_out.reshape(wide, wide_d)
    vmem = pl.BlockSpec(memory_space=pltpu.VMEM)
    smem = pl.BlockSpec(memory_space=pltpu.SMEM)
    anywhere = pl.BlockSpec(memory_space=pl.ANY)
    length = n * tokens

    def attend(groups, tiles, carried, earlier=None, parts=()):
        count = len(tiles)
        carried = carried or [momentum.reshape(wide, wide_d)]
        first = len(carried) == 1
        operands = [tile_mask, *tiles, w_flat, *blocks, *carried, *parts]
        sums = shape((length, wide), F32)
        rows = shape((count * tokens, wide), BF16)
        probs = shape((heads_here, tokens, length), F32)
        scratch = [
            pltpu.VMEM((n, *packed_shape), BF16),
            pltpu.VMEM(rows.shape, BF16),
            pltpu.VMEM((count * tokens, wide_d), BF16),
            pltpu.VMEM((wide, wide_d), BF16),
            pltpu.VMEM(sums.shape, F32),
            pltpu.VMEM(sums.shape, F32),
            pltpu.SemaphoreType.DMA((count + 8 + 2 * n + wide_d // math.gcd(wide_d, 512),)),
        ]
        outs = [rows, sums, sums, rows]
        if earlier is not None:
            outs[0] = shape((n, tokens, wide), BF16)
        out_specs = [vmem] * len(outs)
        if first:
            outs += [probs, shape((tokens, wide), BF16), shape((wide, wide_d), F32)]
            out_specs += [vmem, vmem, anywhere]
            scratch += [pltpu.VMEM((wide, wide_d), F32)]
        flops = count * (14 * tokens * length * wide + 2 * tokens * wide * wide_d)
        return pl.pallas_call(
            functools.partial(
                attend_kernel, n, heads_here, per_group, groups, first, earlier, False
            ),
            in_specs=[smem] + [anywhere] * (len(operands) - 1),
            out_specs=out_specs,
            out_shape=outs,
            scratch_shapes=scratch,
            compiler_params=params(LARGE),
            cost_estimate=cost(flops, count * 2**23),
            name="attend",
        )(*operands)

    waves = waves_of(n)
    early = [[0]] + [[-s, s] for s in range(1, len(waves) + 1)]
    early_tiles, fore, aft = [own], own, own
    for wave in waves:
        fore, aft, *got = lax.optimization_barrier(
            [forward(fore), backward(aft), *[send(packed, k, "seq") for k in wave]]
        )
        early_tiles += [fore, aft]
        for k, block in zip(wave, got):
            blocks[k] = block

    groups, fresh, sums, queries, listed, atts, tiles = early, early_tiles, [], [], [], [], []
    for s in range(len(waves), half):
        if s < half - 1:
            next_fore, next_aft = forward(fore), backward(aft)
            gather = ()
        else:
            far = forward(fore)
            gather = (listed, queries)
        query, key_sum, value_sum, att, *saved = attend(groups, fresh, sums, *gather)
        sums = [key_sum, value_sum]
        if saved:
            far_probs, far_att, part = saved
        else:
            atts.append(att)
            tiles += fresh
        if s < half - 1:
            fore, aft, query, *sums = lax.optimization_barrier(
                [next_fore, next_aft, query, *sums]
            )
            listed.append(sum(groups, []))
            queries.append(query)
            groups, fresh = [[-(s + 1), s + 1]], [fore, aft]
    query_back = lax.all_to_all(query, "seq", split_axis=0, concat_axis=0, tiled=True)
    tile_count = len(tiles)
    rows = (tokens, wide)
    probs_shape = far_probs.shape
    tail_in = [tile_mask, far, w_flat, *blocks, *sums, far_probs, far_att, *atts, *tiles, part]
    far_query, grads, error, *sent = pl.pallas_call(
        functools.partial(tail_kernel, n, heads_here, per_group, workers, tile_count),
        in_specs=[smem] + [anywhere] * (len(tail_in) - 1),
        out_specs=[vmem] + [anywhere] * (2 + workers),
        out_shape=[
            shape(rows, BF16),
            shape((n, 2 * tokens, wide), BF16),
            shape((wide, wide_d), F32),
            *[shape((heads_here, size // workers, wide_d), BF16)] * workers,
        ],
        scratch_shapes=[
            pltpu.VMEM((heads_here, size, wide_d), BF16),
            pltpu.VMEM((tile_count * tokens, wide), BF16),
            pltpu.VMEM((tile_count * tokens, wide_d), BF16),
            pltpu.VMEM((wide, wide_d), F32),
            pltpu.VMEM((wide, wide_d), F32),
            pltpu.SemaphoreType.DMA((2 * tile_count + heads_here * (workers + 2),)),
            pltpu.VMEM((n, *packed_shape), BF16),
            pltpu.VMEM(rows, BF16),
            pltpu.VMEM((tokens, wide_d), BF16),
            pltpu.VMEM((wide, wide_d), BF16),
            pltpu.VMEM((length, wide), F32),
            pltpu.VMEM((length, wide), F32),
            pltpu.SemaphoreType.DMA((n + 8 + heads_here,)),
            pltpu.VMEM(probs_shape, F32),
            pltpu.VMEM(rows, BF16),
            pltpu.VMEM((n, 2 * tokens, wide), BF16),
        ],
        compiler_params=params(LARGE),
        cost_estimate=cost(HEAVY[2], 2**24),
        name="tail",
    )(*tail_in)
    across = [(ring[i], ring[(i + half) % n]) for i in range(n)]
    far_back = lax.ppermute(far_query, "seq", across)
    other_back = lax.all_to_all(grads, "seq", split_axis=0, concat_axis=0, tiled=True)

    received = [sent[0]] + [send(sent, k, "dp") for k in range(1, workers)]

    query_back, far_back, *received = lax.optimization_barrier(
        [query_back, far_back, *received]
    )
    synced, server_error = pl.pallas_call(
        functools.partial(server_kernel, workers),
        out_shape=[
            shape((heads_here, size // workers, wide_d), BF16),
            shape((heads_here, size // workers, wide_d), F32),
        ],
        compiler_params=params(SMALL),
        cost_estimate=cost(HEAVY[0], 2**22),
        name="server",
    )(*received)
    gathered = [synced] + [None] * (workers - 1)
    for k in range(1, workers):
        source, step = (synced, k) if k == 1 or k % 2 == 0 else (gathered[k - 1], 1)
        gathered[k] = lax.ppermute(source, "dp", [(i, i ^ step) for i in range(workers)])

    grad_rows = pl.pallas_call(
        functools.partial(unpack_kernel, n),
        out_shape=shape((3 * tokens, heads, size), BF16),
        in_specs=[anywhere] * 3,
        out_specs=anywhere,
        scratch_shapes=[
            pltpu.VMEM((n, *packed_shape), BF16),
            pltpu.VMEM((tokens, wide), BF16),
            pltpu.VMEM((3 * tokens, heads, size), BF16),
            pltpu.SemaphoreType.DMA((7,)),
        ],
        compiler_params=params(SMALL),
        cost_estimate=cost(0, 4 * qkv.size),
        name="unpack",
    )(query_back, far_back, other_back)
    synced_momentum = pl.pallas_call(
        functools.partial(join_kernel, workers),
        out_shape=shape((heads_here, size, wide_d), BF16),
        compiler_params=params(SMALL),
        cost_estimate=cost(0, 4 * w_out.size),
        name="join",
    )(*gathered)
    return (
        grad_rows.reshape(qkv.shape),
        synced_momentum,
        error.reshape(1, heads_here, size, wide_d),
        server_error,
    )


def solution(mesh):
    placed = (
        P(None, "dp", "seq", None, None),
        P(),
        P("dp", "seq", None),
        P("seq", None, None),
        P("seq", None, None),
    )
    return jax.shard_map(
        body,
        mesh=mesh,
        in_specs=placed,
        out_specs=(
            P(None, "dp", "seq", None, None),
            P("seq", None, None),
            P("dp", "seq", None, None),
            P("seq", "dp", None),
        ),
        check_vma=False,
    )
```

```python
import functools
import math

import jax
import jax.numpy as jnp
from jax import lax
from jax.experimental import pallas as pl
from jax.experimental.pallas import tpu as pltpu
from jax.sharding import PartitionSpec as P

SMALL, LARGE = 16 * 1024 * 1024, 127 * 512 * 1024
F32 = jnp.float32
HEAVY = 10**13, 10**13, 10**13
BF16 = jnp.bfloat16


def params(limit):
    return pltpu.CompilerParams(vmem_limit_bytes=limit)


def cost(flops, moved):
    return pl.CostEstimate(flops=flops, bytes_accessed=moved, transcendentals=0)


def ring_order(n):
    return [i for i in range(n) if i % 2 == 0] + [i for i in reversed(range(n)) if i % 2]


def ring_member(place, n):
    return jnp.where(place < n // 2, 2 * place, 2 * n - 1 - 2 * place)


def ring_place(member, n):
    return jnp.where(member % 2 == 0, member // 2, (2 * n - 1 - member) // 2)


def waves_of(n):
    late = [n - 1] + [k for k in range(n - 2, 1, -1) if k & (k - 1) == 0]
    return [[1] + [k for k in range(n - 2, 1, -1) if k not in late], late]


def dot_nt(a, b):
    return lax.dot_general(a, b, (((1,), (1,)), ((), ())), preferred_element_type=F32)


def dot_tn(a, b):
    return lax.dot_general(a, b, (((0,), (0,)), ((), ())), preferred_element_type=F32)


def pack_kernel(n, x_ref, *refs):
    outs, (x_all, parts, sems) = refs[:n], refs[n:]
    rows, heads, size = x_ref.shape
    wide = heads * size // n
    third = rows // 3
    me = lax.axis_index("seq")
    spans = [pl.ds(i * third, third) for i in range(3)]
    arriving = fetch([(x_ref.at[s], x_all.at[s]) for s in spans], sems)
    leaving = []
    for i, copy in enumerate(arriving):
        copy.wait()
        here = slice(i * third, (i + 1) * third)
        x = x_all[here].reshape(third, heads * size)
        for d in range(n):
            parts[d, here] = x[:, d * wide : (d + 1) * wide]
        going = [(parts.at[me ^ k, spans[i]], outs[k].at[spans[i]]) for k in range(n)]
        leaving += fetch(going, sems, 3 + i * n)
    for copy in leaving:
        copy.wait()


def unpack_kernel(n, queries_ref, far_ref, others_ref, out_ref, blocks, far_all, rows, sems):
    tokens = far_ref.shape[0]
    me = lax.axis_index("seq")
    spans = [pl.ds(i * tokens, tokens) for i in range(3)]
    copies = fetch(
        [(queries_ref, blocks.at[:, spans[0]]), (far_ref, far_all)]
        + [(others_ref.at[:, spans[i]], blocks.at[:, spans[i + 1]]) for i in range(2)],
        sems,
    )
    copies.pop(0).wait()
    leaving = []
    for i, copy in enumerate(copies):
        copy.wait()
        here = slice(i * tokens, (i + 1) * tokens)
        if i == 0:
            far_place = ring_member(lax.rem(ring_place(me, n) + n // 2, n), n)
            blocks[far_place, here] = far_all[...]
        joined = jnp.concatenate([blocks[d, here] for d in range(n)], axis=1)
        rows[here] = joined.reshape(tokens, *rows.shape[1:])
        leaving += fetch([(rows.at[spans[i]], out_ref.at[spans[i]])], sems, 4 + i)
    for copy in leaving:
        copy.wait()


def fetch(copies, sems, first=0):
    started = [
        pltpu.make_async_copy(source, target, sems.at[first + i])
        for i, (source, target) in enumerate(copies)
    ]
    for copy in started:
        copy.start()
    return started


def rows_of(tiles, buffer):
    copies, start = [], 0
    for tile in tiles:
        copies.append((tile, buffer.at[pl.ds(start, tile.shape[0])]))
        start += tile.shape[0]
    return copies


def attend_kernel(n, heads_here, per_group, groups, first, earlier, far, mask_ref, *refs, beside=None):
    refs = list(refs)
    count = sum(len(g) for g in groups)
    take = lambda m: [refs.pop(0) for _ in range(m)]
    tiles = take(count)
    (w_ref,) = take(1)
    blocks = take(n)
    carried = [] if first else take(2)
    (mom_ref,) = take(1) if first else [None]
    query_parts = [] if earlier is None else take(len(earlier))
    if far:
        far_probs_ref, far_att_ref, query_out, grads_out = take(4)
    else:
        query_out, key_out, value_out, att_out = take(4)
    if first:
        far_probs_out, far_att_out, part_out = take(3)
    qkv_all, cot_all, tile_all, w_all, key_all, value_all, sems = take(7)
    if far:
        far_probs, far_att, grads = take(3)
    if first:
        (mom_all,) = take(1)

    me = lax.axis_index("seq")
    sign = 1 - 2 * lax.rem(lax.axis_index("dp"), 2)
    wide = qkv_all.shape[2]
    tokens = qkv_all.shape[1] // 3
    size = wide // heads_here
    length = n * tokens
    queries_of = lambda ids, cols: jnp.concatenate([qkv_all[t, 0:tokens, cols] for t in ids], axis=0)
    keys_of = lambda cols: qkv_all[:, tokens : 2 * tokens, cols].reshape(length, size)
    values_of = lambda cols: qkv_all[:, 2 * tokens :, cols].reshape(length, size)
    inv_root = 1.0 / math.sqrt(size)
    place = ring_place(me, n)
    tile_of = lambda offset: ring_member(lax.rem(place + sign * offset + n, n), n)

    used = 0

    def start(copies):
        nonlocal used
        used += len(copies)
        return fetch(copies, sems, used - len(copies))

    w_copy, *tile_copies = start([(w_ref, w_all), *rows_of(tiles, tile_all)])
    att_copies = start([(far_att_ref, far_att)] if far else [])
    work = beside(tile_all, far_att) if beside else None
    far_copies = start([(far_probs_ref, far_probs)] if far else [])
    block_copies = start([(block, qkv_all.at[me ^ k]) for k, block in enumerate(blocks)])
    carried_copies = start(list(zip(carried, (key_all, value_all))))
    mom_copies = start([(mom_ref, mom_all)] if first else [])
    part_copies = start(
        [
            (part.at[pl.ds(i * tokens, tokens)], query_out.at[tile_of(offset)])
            for part, offsets in zip(query_parts, earlier or [])
            for i, offset in enumerate(offsets)
        ]
    )
    leaving = []
    if earlier is not None:
        query_out[tile_of(n // 2)] = jnp.zeros((tokens, wide), BF16)

    def forward(ids, h):
        cols = slice(h * size, (h + 1) * size)
        kind = (me * heads_here + h) // per_group
        bias = [
            jnp.concatenate(
                [
                    jnp.full(
                        (1, tokens), jnp.where(mask_ref[kind, t, k] == 1, 0.0, -jnp.inf), F32
                    )
                    for k in range(n)
                ],
                axis=1,
            )
            for t in ids
        ]
        bias = jnp.concatenate([jnp.broadcast_to(b, (tokens, length)) for b in bias], axis=0)
        scores = dot_nt(queries_of(ids, cols), keys_of(cols)) * inv_root + bias
        expo = jnp.exp(scores - jnp.max(scores, axis=1, keepdims=True))
        probs = expo * (1.0 / jnp.sum(expo, axis=1, keepdims=True))
        att = jnp.dot(probs.astype(BF16), values_of(cols), preferred_element_type=F32).astype(BF16)
        return probs, att

    w_copy.wait()
    begin = 0
    for number, group in enumerate(groups):
        ids = [tile_of(offset) for offset in group]
        rows = slice(begin, begin + len(ids) * tokens)
        begin += len(ids) * tokens
        for copy in tile_copies[: len(ids)]:
            copy.wait()
        tile_copies = tile_copies[len(ids) :]
        cot_all[rows] = dot_nt(tile_all[rows], w_all[...]).astype(BF16)
        if work:
            att_copies.pop().wait()
            leaving += work()
        if number == 0:
            for copy in block_copies + far_copies:
                copy.wait()
        for h in range(heads_here):
            cols = slice(h * size, (h + 1) * size)
            if far:
                probs, att = far_probs[h], far_att[:, cols]
            else:
                probs, att = forward(ids, h)
                att_out[rows, cols] = att
            probs_b = probs.astype(BF16)
            cot = cot_all[rows, cols]
            delta = jnp.sum(cot.astype(F32) * att.astype(F32), axis=1, keepdims=True)
            dprobs = dot_nt(cot, values_of(cols))
            dscores = (probs * (dprobs - delta)).astype(BF16)
            query_grad = jnp.dot(dscores, keys_of(cols), preferred_element_type=F32) * inv_root
            query_grad = query_grad.astype(BF16)
            if earlier is None:
                query_out[rows, cols] = query_grad
            else:
                for i, t in enumerate(ids):
                    query_out[t, :, cols] = query_grad[i * tokens : (i + 1) * tokens]
            key_sum = dot_tn(dscores, queries_of(ids, cols))
            value_sum = dot_tn(probs_b, cot)
            if number == 0 and h == 0:
                for copy in carried_copies:
                    copy.wait()
            if number > 0 or not first:
                key_sum = key_all[:, cols] + key_sum
                value_sum = value_all[:, cols] + value_sum
            if far:
                grads[:, 0:tokens, cols] = (
                    (key_sum * inv_root).astype(BF16).reshape(n, tokens, size)
                )
                grads[:, tokens:, cols] = value_sum.astype(BF16).reshape(n, tokens, size)
                span = pl.ds(h * size, size)
                leaving += start([(grads.at[:, :, span], grads_out.at[:, :, span])])
            elif number == len(groups) - 1:
                key_out[:, cols] = key_sum
                value_out[:, cols] = value_sum
            else:
                key_all[:, cols] = key_sum
                value_all[:, cols] = value_sum
    if first:
        for h in range(heads_here):
            probs, att = forward([tile_of(n // 2)], h)
            far_probs_out[h] = probs
            far_att_out[:, h * size : (h + 1) * size] = att
        for copy in mom_copies:
            copy.wait()
        wide_d = mom_all.shape[1]
        chunk = math.gcd(wide_d, 512)
        att = att_out[...].T
        for c in range(0, wide_d, chunk):
            cols = slice(c, c + chunk)
            grad = jnp.dot(att, tile_all[:, cols], preferred_element_type=F32)
            mom_all[:, cols] = 0.9 * mom_all[:, cols] + 0.1 * grad
            span = pl.ds(c, chunk)
            leaving += start([(mom_all.at[:, span], part_out.at[:, span])])
    for copy in part_copies + leaving:
        copy.wait()


def tail_kernel(n, heads_here, per_group, workers, tile_count, *refs):
    refs = list(refs)
    take = lambda m: [refs.pop(0) for _ in range(m)]
    attend_in = take(1 + 2 + n + 2 + 2)
    att_parts, tiles, (part_ref,) = take(tile_count // 2), take(tile_count), take(1)
    attend_out, (error_ref,), outs = take(2), take(1), take(workers)
    sent_ref, att_all, more_tiles, mom_all, error_all, worker_sems, *attend_scratch = refs

    def beside(far_tile, far_att):
        wide, wide_d = mom_all.shape
        size = wide // heads_here
        chunk = math.gcd(wide_d, 512)
        block = size // workers
        spans = [pl.ds(h * size, size) for h in range(heads_here)]
        copies = [*rows_of(att_parts, att_all), *rows_of(tiles, more_tiles)]
        copies = fetch(copies, worker_sems)
        mom_copies = fetch(
            [(part_ref.at[s], mom_all.at[s]) for s in spans], worker_sems, len(copies)
        )
        used = len(copies) + heads_here

        def work():
            for copy in copies:
                copy.wait()
            att, late = att_all[...].T, far_att[...].T
            leaving = []
            for h in range(heads_here):
                rows = slice(h * size, (h + 1) * size)
                mom_copies[h].wait()
                total = jnp.zeros((size, chunk), F32)
                for c in range(0, wide_d, chunk):
                    cols = slice(c, c + chunk)
                    grad = jnp.dot(att[rows], more_tiles[:, cols], preferred_element_type=F32)
                    grad += jnp.dot(late[rows], far_tile[:, cols], preferred_element_type=F32)
                    mom = mom_all[rows, cols] + 0.1 * grad
                    mom_all[rows, cols] = mom
                    total = total + jnp.abs(mom)
                scale = jnp.sum(total, keepdims=True) * (1.0 / (size * wide_d)) + 1e-06
                inverse = 1.0 / scale
                for c in range(0, wide_d, chunk):
                    cols = slice(c, c + chunk)
                    mom = mom_all[rows, cols]
                    sent = (scale * jnp.tanh(mom * inverse)).astype(BF16)
                    sent_ref[h, :, cols] = sent
                    error_all[rows, cols] = mom - sent.astype(F32)
                me = lax.axis_index("dp")
                going = [(error_all.at[spans[h]], error_ref.at[spans[h]])]
                for k in range(workers):
                    start = pl.multiple_of((me ^ k) * block, block)
                    going.append((sent_ref.at[h, pl.ds(start, block)], outs[k].at[h]))
                leaving.extend(fetch(going, worker_sems, used + h * len(going)))
            return leaving

        return work

    attend_kernel(
        n, heads_here, per_group, [[n // 2]], False, None, True,
        *attend_in, *attend_out, *attend_scratch, beside=beside,
    )


def server_kernel(workers, *refs):
    blocks, synced_ref, error_ref = refs[:workers], refs[workers], refs[workers + 1]
    heads_here, block, wide_d = synced_ref.shape
    for h in range(heads_here):
        total = blocks[0][h].astype(F32)
        for k in range(1, workers):
            total = total + blocks[k][h].astype(F32)
        averaged = total * (1.0 / workers)
        scale = jnp.sum(jnp.abs(averaged), keepdims=True) * (1.0 / (block * wide_d)) + 1e-06
        synced = (scale * jnp.tanh(averaged * (1.0 / scale))).astype(BF16)
        synced_ref[h] = synced
        error_ref[h] = averaged - synced.astype(F32)


def join_kernel(workers, *refs):
    blocks, out_ref = refs[:workers], refs[workers]
    me = lax.axis_index("dp")
    block = blocks[0].shape[1]
    for k in range(workers):
        start = pl.multiple_of((me ^ k) * block, block)
        out_ref[:, pl.ds(start, block), :] = blocks[k][...]


def body(qkv, tile_mask, d_out, w_out, momentum):
    n = lax.axis_size("seq")
    workers = lax.axis_size("dp")
    tokens, heads, size = qkv.shape[2:]
    heads_here = w_out.shape[0]
    groups = tile_mask.shape[0]
    per_group = heads // groups
    wide = heads_here * size
    wide_d = d_out.shape[2]
    half = n // 2
    shape = jax.ShapeDtypeStruct

    vmem = pl.BlockSpec(memory_space=pltpu.VMEM)
    smem = pl.BlockSpec(memory_space=pltpu.SMEM)
    anywhere = pl.BlockSpec(memory_space=pl.ANY)
    ring = ring_order(n)

    def around(turn):
        pairs = []
        for worker in range(workers):
            way = turn if worker % 2 == 0 else -turn
            pairs += [(worker * n + ring[i], worker * n + ring[(i + way) % n]) for i in range(n)]
        return lambda x: lax.ppermute(x, ("dp", "seq"), pairs)

    forward, backward = around(1), around(-1)
    own = d_out[0]
    packed_shape = (3 * tokens, wide)
    packed = pl.pallas_call(
        functools.partial(pack_kernel, n),
        in_specs=[anywhere],
        out_specs=[anywhere] * n,
        out_shape=[shape(packed_shape, BF16)] * n,
        scratch_shapes=[
            pltpu.VMEM((3 * tokens, heads, size), BF16),
            pltpu.VMEM((n, *packed_shape), BF16),
            pltpu.SemaphoreType.DMA((3 + 3 * n,)),
        ],
        compiler_params=params(LARGE),
        cost_estimate=cost(0, 4 * qkv.size),
        name="pack",
    )(qkv.reshape(3 * tokens, heads, size))

    def send(blocks, k, axis):
        return lax.ppermute(blocks[k], axis, [(i, i ^ k) for i in range(len(blocks))])

    blocks = list(packed)
    w_flat = w_out.reshape(wide, wide_d)
    length = n * tokens

    def attend(groups, tiles, carried, earlier=None, parts=()):
        count = len(tiles)
        carried = carried or [momentum.reshape(wide, wide_d)]
        first = len(carried) == 1
        operands = [tile_mask, *tiles, w_flat, *blocks, *carried, *parts]
        sums = shape((length, wide), F32)
        rows = shape((count * tokens, wide), BF16)
        probs = shape((heads_here, tokens, length), F32)
        scratch = [
            pltpu.VMEM((n, *packed_shape), BF16),
            pltpu.VMEM(rows.shape, BF16),
            pltpu.VMEM((count * tokens, wide_d), BF16),
            pltpu.VMEM((wide, wide_d), BF16),
            pltpu.VMEM(sums.shape, F32),
            pltpu.VMEM(sums.shape, F32),
            pltpu.SemaphoreType.DMA((count + 8 + 2 * n + wide_d // math.gcd(wide_d, 512),)),
        ]
        outs = [rows, sums, sums, rows]
        if earlier is not None:
            outs[0] = shape((n, tokens, wide), BF16)
        out_specs = [vmem] * len(outs)
        if first:
            outs += [probs, shape((tokens, wide), BF16), shape((wide, wide_d), F32)]
            out_specs += [vmem, vmem, anywhere]
            scratch += [pltpu.VMEM((wide, wide_d), F32)]
        flops = count * (14 * tokens * length * wide + 2 * tokens * wide * wide_d)
        return pl.pallas_call(
            functools.partial(
                attend_kernel, n, heads_here, per_group, groups, first, earlier, False
            ),
            in_specs=[smem] + [anywhere] * (len(operands) - 1),
            out_specs=out_specs,
            out_shape=outs,
            scratch_shapes=scratch,
            compiler_params=params(LARGE),
            cost_estimate=cost(flops, count * 2**23),
            name="attend",
        )(*operands)

    waves = waves_of(n)
    early = [[0]] + [[-s, s] for s in range(1, len(waves) + 1)]
    early_tiles, fore, aft = [own], own, own
    for wave in waves:
        fore, aft, *got = lax.optimization_barrier(
            [forward(fore), backward(aft), *[send(packed, k, "seq") for k in wave]]
        )
        early_tiles += [fore, aft]
        for k, block in zip(wave, got):
            blocks[k] = block

    groups, fresh, sums, queries, listed, atts, tiles = early, early_tiles, [], [], [], [], []
    for s in range(len(waves), half):
        if s < half - 1:
            next_fore, next_aft = forward(fore), backward(aft)
            gather = ()
        else:
            far = forward(fore)
            gather = (listed, queries)
        query, key_sum, value_sum, att, *saved = attend(groups, fresh, sums, *gather)
        sums = [key_sum, value_sum]
        if saved:
            far_probs, far_att, part = saved
        else:
            atts.append(att)
            tiles += fresh
        if s < half - 1:
            fore, aft, query, *sums = lax.optimization_barrier(
                [next_fore, next_aft, query, *sums]
            )
            listed.append(sum(groups, []))
            queries.append(query)
            groups, fresh = [[-(s + 1), s + 1]], [fore, aft]
    query_back = lax.all_to_all(query, "seq", split_axis=0, concat_axis=0, tiled=True)
    tile_count = len(tiles)
    rows = (tokens, wide)
    probs_shape = far_probs.shape
    tail_in = [tile_mask, far, w_flat, *blocks, *sums, far_probs, far_att, *atts, *tiles, part]
    far_query, grads, error, *sent = pl.pallas_call(
        functools.partial(tail_kernel, n, heads_here, per_group, workers, tile_count),
        in_specs=[smem] + [anywhere] * (len(tail_in) - 1),
        out_specs=[vmem] + [anywhere] * (2 + workers),
        out_shape=[
            shape(rows, BF16),
            shape((n, 2 * tokens, wide), BF16),
            shape((wide, wide_d), F32),
            *[shape((heads_here, size // workers, wide_d), BF16)] * workers,
        ],
        scratch_shapes=[
            pltpu.VMEM((heads_here, size, wide_d), BF16),
            pltpu.VMEM((tile_count * tokens, wide), BF16),
            pltpu.VMEM((tile_count * tokens, wide_d), BF16),
            pltpu.VMEM((wide, wide_d), F32),
            pltpu.VMEM((wide, wide_d), F32),
            pltpu.SemaphoreType.DMA((2 * tile_count + heads_here * (workers + 2),)),
            pltpu.VMEM((n, *packed_shape), BF16),
            pltpu.VMEM(rows, BF16),
            pltpu.VMEM((tokens, wide_d), BF16),
            pltpu.VMEM((wide, wide_d), BF16),
            pltpu.VMEM((length, wide), F32),
            pltpu.VMEM((length, wide), F32),
            pltpu.SemaphoreType.DMA((n + 8 + heads_here,)),
            pltpu.VMEM(probs_shape, F32),
            pltpu.VMEM(rows, BF16),
            pltpu.VMEM((n, 2 * tokens, wide), BF16),
        ],
        compiler_params=params(LARGE),
        cost_estimate=cost(HEAVY[2], 2**24),
        name="tail",
    )(*tail_in)
    across = [(ring[i], ring[(i + half) % n]) for i in range(n)]
    far_back = lax.ppermute(far_query, "seq", across)
    other_back = lax.all_to_all(grads, "seq", split_axis=0, concat_axis=0, tiled=True)

    received = [sent[0]] + [send(sent, k, "dp") for k in range(1, workers)]

    query_back, far_back, *received = lax.optimization_barrier(
        [query_back, far_back, *received]
    )
    synced, server_error = pl.pallas_call(
        functools.partial(server_kernel, workers),
        out_shape=[
            shape((heads_here, size // workers, wide_d), BF16),
            shape((heads_here, size // workers, wide_d), F32),
        ],
        compiler_params=params(SMALL),
        cost_estimate=cost(HEAVY[0], 2**22),
        name="server",
    )(*received)
    gathered = [synced] + [None] * (workers - 1)
    for k in range(1, workers):
        source, step = (synced, k) if k == 1 or k % 2 == 0 else (gathered[k - 1], 1)
        gathered[k] = lax.ppermute(source, "dp", [(i, i ^ step) for i in range(workers)])

    grad_rows = pl.pallas_call(
        functools.partial(unpack_kernel, n),
        out_shape=shape((3 * tokens, heads, size), BF16),
        in_specs=[anywhere] * 3,
        out_specs=anywhere,
        scratch_shapes=[
            pltpu.VMEM((n, *packed_shape), BF16),
            pltpu.VMEM((tokens, wide), BF16),
            pltpu.VMEM((3 * tokens, heads, size), BF16),
            pltpu.SemaphoreType.DMA((7,)),
        ],
        compiler_params=params(SMALL),
        cost_estimate=cost(0, 4 * qkv.size),
        name="unpack",
    )(query_back, far_back, other_back)
    synced_momentum = pl.pallas_call(
        functools.partial(join_kernel, workers),
        out_shape=shape((heads_here, size, wide_d), BF16),
        compiler_params=params(SMALL),
        cost_estimate=cost(0, 4 * w_out.size),
        name="join",
    )(*gathered)
    return (
        grad_rows.reshape(qkv.shape),
        synced_momentum,
        error.reshape(1, heads_here, size, wide_d),
        server_error,
    )


def solution(mesh):
    placed = (
        P(None, "dp", "seq", None, None),
        P(),
        P("dp", "seq", None),
        P("seq", None, None),
        P("seq", None, None),
    )
    return jax.shard_map(
        body,
        mesh=mesh,
        in_specs=placed,
        out_specs=(
            P(None, "dp", "seq", None, None),
            P("seq", None, None),
            P("dp", "seq", None, None),
            P("seq", "dp", None),
        ),
        check_vma=False,
    )
```

```python
import functools
import math

import jax
import jax.numpy as jnp
from jax import lax
from jax.experimental import pallas as pl
from jax.experimental.pallas import tpu as pltpu
from jax.sharding import PartitionSpec as P

SMALL, LARGE = 16 * 1024 * 1024, 127 * 512 * 1024
F32 = jnp.float32
HEAVY = 10**13, 10**13, 10**13
BF16 = jnp.bfloat16


def params(limit):
    return pltpu.CompilerParams(vmem_limit_bytes=limit)


def cost(flops, moved):
    return pl.CostEstimate(flops=flops, bytes_accessed=moved, transcendentals=0)


def ring_order(n):
    return [i for i in range(n) if i % 2 == 0] + [i for i in reversed(range(n)) if i % 2]


def ring_member(place, n):
    return jnp.where(place < n // 2, 2 * place, 2 * n - 1 - 2 * place)


def ring_place(member, n):
    return jnp.where(member % 2 == 0, member // 2, (2 * n - 1 - member) // 2)


def waves_of(n):
    late = [n - 1] + [k for k in range(n - 2, 1, -1) if k & (k - 1) == 0]
    early = [1] + [k for k in range(n - 2, 1, -1) if k not in late]
    return [early, late[:1] + late[:0:-1]]


def dot_nt(a, b):
    return lax.dot_general(a, b, (((1,), (1,)), ((), ())), preferred_element_type=F32)


def dot_tn(a, b):
    return lax.dot_general(a, b, (((0,), (0,)), ((), ())), preferred_element_type=F32)


def pack_kernel(n, x_ref, *refs):
    outs, (x_all, parts, sems) = refs[:n], refs[n:]
    rows, heads, size = x_ref.shape
    wide = heads * size // n
    third = rows // 3
    me = lax.axis_index("seq")
    spans = [pl.ds(i * third, third) for i in range(3)]
    arriving = fetch([(x_ref.at[s], x_all.at[s]) for s in spans], sems)
    leaving = []
    for i, copy in enumerate(arriving):
        copy.wait()
        here = slice(i * third, (i + 1) * third)
        x = x_all[here].reshape(third, heads * size)
        for d in range(n):
            parts[d, here] = x[:, d * wide : (d + 1) * wide]
        going = [(parts.at[me ^ k, spans[i]], outs[k].at[spans[i]]) for k in range(n)]
        leaving += fetch(going, sems, 3 + i * n)
    for copy in leaving:
        copy.wait()


def unpack_kernel(n, queries_ref, far_ref, others_ref, out_ref, blocks, far_all, rows, sems):
    tokens = far_ref.shape[0]
    me = lax.axis_index("seq")
    spans = [pl.ds(i * tokens, tokens) for i in range(3)]
    copies = fetch(
        [(queries_ref, blocks.at[:, spans[0]]), (far_ref, far_all)]
        + [(others_ref.at[:, spans[i]], blocks.at[:, spans[i + 1]]) for i in range(2)],
        sems,
    )
    copies.pop(0).wait()
    leaving = []
    for i, copy in enumerate(copies):
        copy.wait()
        here = slice(i * tokens, (i + 1) * tokens)
        if i == 0:
            far_place = ring_member(lax.rem(ring_place(me, n) + n // 2, n), n)
            blocks[far_place, here] = far_all[...]
        joined = jnp.concatenate([blocks[d, here] for d in range(n)], axis=1)
        rows[here] = joined.reshape(tokens, *rows.shape[1:])
        leaving += fetch([(rows.at[spans[i]], out_ref.at[spans[i]])], sems, 4 + i)
    for copy in leaving:
        copy.wait()


def fetch(copies, sems, first=0):
    started = [
        pltpu.make_async_copy(source, target, sems.at[first + i])
        for i, (source, target) in enumerate(copies)
    ]
    for copy in started:
        copy.start()
    return started


def rows_of(tiles, buffer):
    copies, start = [], 0
    for tile in tiles:
        copies.append((tile, buffer.at[pl.ds(start, tile.shape[0])]))
        start += tile.shape[0]
    return copies


def attend_kernel(n, heads_here, per_group, groups, first, earlier, far, mask_ref, *refs, beside=None):
    refs = list(refs)
    count = sum(len(g) for g in groups)
    take = lambda m: [refs.pop(0) for _ in range(m)]
    tiles = take(count)
    (w_ref,) = take(1)
    blocks = take(n)
    carried = [] if first else take(2)
    (mom_ref,) = take(1) if first else [None]
    query_parts = [] if earlier is None else take(len(earlier))
    if far:
        far_probs_ref, far_att_ref, query_out, grads_out = take(4)
    else:
        query_out, key_out, value_out, att_out = take(4)
    if first:
        far_probs_out, far_att_out, part_out = take(3)
    qkv_all, cot_all, tile_all, w_all, key_all, value_all, sems = take(7)
    if far:
        far_probs, far_att, grads = take(3)
    if first:
        (mom_all,) = take(1)

    me = lax.axis_index("seq")
    sign = 1 - 2 * lax.rem(lax.axis_index("dp"), 2)
    wide = qkv_all.shape[2]
    tokens = qkv_all.shape[1] // 3
    size = wide // heads_here
    length = n * tokens
    queries_of = lambda ids, cols: jnp.concatenate([qkv_all[t, 0:tokens, cols] for t in ids], axis=0)
    keys_of = lambda cols: qkv_all[:, tokens : 2 * tokens, cols].reshape(length, size)
    values_of = lambda cols: qkv_all[:, 2 * tokens :, cols].reshape(length, size)
    inv_root = 1.0 / math.sqrt(size)
    place = ring_place(me, n)
    tile_of = lambda offset: ring_member(lax.rem(place + sign * offset + n, n), n)

    used = 0

    def start(copies):
        nonlocal used
        used += len(copies)
        return fetch(copies, sems, used - len(copies))

    w_copy, *tile_copies = start([(w_ref, w_all), *rows_of(tiles, tile_all)])
    att_copies = start([(far_att_ref, far_att)] if far else [])
    work = beside(tile_all, far_att) if beside else None
    far_copies = start([(far_probs_ref, far_probs)] if far else [])
    block_copies = start([(block, qkv_all.at[me ^ k]) for k, block in enumerate(blocks)])
    carried_copies = start(list(zip(carried, (key_all, value_all))))
    mom_copies = start([(mom_ref, mom_all)] if first else [])
    part_copies = start(
        [
            (part.at[pl.ds(i * tokens, tokens)], query_out.at[tile_of(offset)])
            for part, offsets in zip(query_parts, earlier or [])
            for i, offset in enumerate(offsets)
        ]
    )
    leaving = []
    if earlier is not None:
        query_out[tile_of(n // 2)] = jnp.zeros((tokens, wide), BF16)

    def forward(ids, h):
        cols = slice(h * size, (h + 1) * size)
        kind = (me * heads_here + h) // per_group
        bias = [
            jnp.concatenate(
                [
                    jnp.full(
                        (1, tokens), jnp.where(mask_ref[kind, t, k] == 1, 0.0, -jnp.inf), F32
                    )
                    for k in range(n)
                ],
                axis=1,
            )
            for t in ids
        ]
        bias = jnp.concatenate([jnp.broadcast_to(b, (tokens, length)) for b in bias], axis=0)
        scores = dot_nt(queries_of(ids, cols), keys_of(cols)) * inv_root + bias
        expo = jnp.exp(scores - jnp.max(scores, axis=1, keepdims=True))
        probs = expo * (1.0 / jnp.sum(expo, axis=1, keepdims=True))
        att = jnp.dot(probs.astype(BF16), values_of(cols), preferred_element_type=F32).astype(BF16)
        return probs, att

    w_copy.wait()
    begin = 0
    for number, group in enumerate(groups):
        ids = [tile_of(offset) for offset in group]
        rows = slice(begin, begin + len(ids) * tokens)
        begin += len(ids) * tokens
        for copy in tile_copies[: len(ids)]:
            copy.wait()
        tile_copies = tile_copies[len(ids) :]
        cot_all[rows] = dot_nt(tile_all[rows], w_all[...]).astype(BF16)
        if work:
            att_copies.pop().wait()
            leaving += work()
        if number == 0:
            for copy in block_copies + far_copies:
                copy.wait()
        for h in range(heads_here):
            cols = slice(h * size, (h + 1) * size)
            if far:
                probs, att = far_probs[h], far_att[:, cols]
            else:
                probs, att = forward(ids, h)
                att_out[rows, cols] = att
            probs_b = probs.astype(BF16)
            cot = cot_all[rows, cols]
            delta = jnp.sum(cot.astype(F32) * att.astype(F32), axis=1, keepdims=True)
            dprobs = dot_nt(cot, values_of(cols))
            dscores = (probs * (dprobs - delta)).astype(BF16)
            query_grad = jnp.dot(dscores, keys_of(cols), preferred_element_type=F32) * inv_root
            query_grad = query_grad.astype(BF16)
            if earlier is None:
                query_out[rows, cols] = query_grad
            else:
                for i, t in enumerate(ids):
                    query_out[t, :, cols] = query_grad[i * tokens : (i + 1) * tokens]
            key_sum = dot_tn(dscores, queries_of(ids, cols))
            value_sum = dot_tn(probs_b, cot)
            if number == 0 and h == 0:
                for copy in carried_copies:
                    copy.wait()
            if number > 0 or not first:
                key_sum = key_all[:, cols] + key_sum
                value_sum = value_all[:, cols] + value_sum
            if far:
                grads[:, 0:tokens, cols] = (
                    (key_sum * inv_root).astype(BF16).reshape(n, tokens, size)
                )
                grads[:, tokens:, cols] = value_sum.astype(BF16).reshape(n, tokens, size)
                span = pl.ds(h * size, size)
                leaving += start([(grads.at[:, :, span], grads_out.at[:, :, span])])
            elif number == len(groups) - 1:
                key_out[:, cols] = key_sum
                value_out[:, cols] = value_sum
            else:
                key_all[:, cols] = key_sum
                value_all[:, cols] = value_sum
    if first:
        for h in range(heads_here):
            probs, att = forward([tile_of(n // 2)], h)
            far_probs_out[h] = probs
            far_att_out[:, h * size : (h + 1) * size] = att
        for copy in mom_copies:
            copy.wait()
        wide_d = mom_all.shape[1]
        chunk = math.gcd(wide_d, 512)
        att = att_out[...].T
        for c in range(0, wide_d, chunk):
            cols = slice(c, c + chunk)
            grad = jnp.dot(att, tile_all[:, cols], preferred_element_type=F32)
            mom_all[:, cols] = 0.9 * mom_all[:, cols] + 0.1 * grad
            span = pl.ds(c, chunk)
            leaving += start([(mom_all.at[:, span], part_out.at[:, span])])
    for copy in part_copies + leaving:
        copy.wait()


def tail_kernel(n, heads_here, per_group, workers, tile_count, *refs):
    refs = list(refs)
    take = lambda m: [refs.pop(0) for _ in range(m)]
    attend_in = take(1 + 2 + n + 2 + 2)
    att_parts, tiles, (part_ref,) = take(tile_count // 2), take(tile_count), take(1)
    attend_out, (error_ref,), outs = take(2), take(1), take(workers)
    sent_ref, att_all, more_tiles, mom_all, error_all, worker_sems, *attend_scratch = refs

    def beside(far_tile, far_att):
        wide, wide_d = mom_all.shape
        size = wide // heads_here
        chunk = math.gcd(wide_d, 512)
        block = size // workers
        spans = [pl.ds(h * size, size) for h in range(heads_here)]
        copies = [*rows_of(att_parts, att_all), *rows_of(tiles, more_tiles)]
        copies = fetch(copies, worker_sems)
        mom_copies = fetch(
            [(part_ref.at[s], mom_all.at[s]) for s in spans], worker_sems, len(copies)
        )
        used = len(copies) + heads_here

        def work():
            for copy in copies:
                copy.wait()
            att, late = att_all[...].T, far_att[...].T
            leaving = []
            for h in range(heads_here):
                rows = slice(h * size, (h + 1) * size)
                mom_copies[h].wait()
                total = jnp.zeros((size, chunk), F32)
                for c in range(0, wide_d, chunk):
                    cols = slice(c, c + chunk)
                    grad = jnp.dot(att[rows], more_tiles[:, cols], preferred_element_type=F32)
                    grad += jnp.dot(late[rows], far_tile[:, cols], preferred_element_type=F32)
                    mom = mom_all[rows, cols] + 0.1 * grad
                    mom_all[rows, cols] = mom
                    total = total + jnp.abs(mom)
                scale = jnp.sum(total, keepdims=True) * (1.0 / (size * wide_d)) + 1e-06
                inverse = 1.0 / scale
                for c in range(0, wide_d, chunk):
                    cols = slice(c, c + chunk)
                    mom = mom_all[rows, cols]
                    sent = (scale * jnp.tanh(mom * inverse)).astype(BF16)
                    sent_ref[h, :, cols] = sent
                    error_all[rows, cols] = mom - sent.astype(F32)
                me = lax.axis_index("dp")
                going = [(error_all.at[spans[h]], error_ref.at[spans[h]])]
                for k in range(workers):
                    start = pl.multiple_of((me ^ k) * block, block)
                    going.append((sent_ref.at[h, pl.ds(start, block)], outs[k].at[h]))
                leaving.extend(fetch(going, worker_sems, used + h * len(going)))
            return leaving

        return work

    attend_kernel(
        n, heads_here, per_group, [[n // 2]], False, None, True,
        *attend_in, *attend_out, *attend_scratch, beside=beside,
    )


def server_kernel(workers, *refs):
    blocks, synced_ref, error_ref = refs[:workers], refs[workers], refs[workers + 1]
    heads_here, block, wide_d = synced_ref.shape
    for h in range(heads_here):
        total = blocks[0][h].astype(F32)
        for k in range(1, workers):
            total = total + blocks[k][h].astype(F32)
        averaged = total * (1.0 / workers)
        scale = jnp.sum(jnp.abs(averaged), keepdims=True) * (1.0 / (block * wide_d)) + 1e-06
        synced = (scale * jnp.tanh(averaged * (1.0 / scale))).astype(BF16)
        synced_ref[h] = synced
        error_ref[h] = averaged - synced.astype(F32)


def join_kernel(workers, *refs):
    blocks, out_ref = refs[:workers], refs[workers]
    me = lax.axis_index("dp")
    block = blocks[0].shape[1]
    for k in range(workers):
        start = pl.multiple_of((me ^ k) * block, block)
        out_ref[:, pl.ds(start, block), :] = blocks[k][...]


def body(qkv, tile_mask, d_out, w_out, momentum):
    n = lax.axis_size("seq")
    workers = lax.axis_size("dp")
    tokens, heads, size = qkv.shape[2:]
    heads_here = w_out.shape[0]
    groups = tile_mask.shape[0]
    per_group = heads // groups
    wide = heads_here * size
    wide_d = d_out.shape[2]
    half = n // 2
    shape = jax.ShapeDtypeStruct

    vmem = pl.BlockSpec(memory_space=pltpu.VMEM)
    smem = pl.BlockSpec(memory_space=pltpu.SMEM)
    anywhere = pl.BlockSpec(memory_space=pl.ANY)
    ring = ring_order(n)

    def around(turn):
        pairs = []
        for worker in range(workers):
            way = turn if worker % 2 == 0 else -turn
            pairs += [(worker * n + ring[i], worker * n + ring[(i + way) % n]) for i in range(n)]
        return lambda x: lax.ppermute(x, ("dp", "seq"), pairs)

    forward, backward = around(1), around(-1)
    own = d_out[0]
    packed_shape = (3 * tokens, wide)
    packed = pl.pallas_call(
        functools.partial(pack_kernel, n),
        in_specs=[anywhere],
        out_specs=[anywhere] * n,
        out_shape=[shape(packed_shape, BF16)] * n,
        scratch_shapes=[
            pltpu.VMEM((3 * tokens, heads, size), BF16),
            pltpu.VMEM((n, *packed_shape), BF16),
            pltpu.SemaphoreType.DMA((3 + 3 * n,)),
        ],
        compiler_params=params(LARGE),
        cost_estimate=cost(0, 4 * qkv.size),
        name="pack",
    )(qkv.reshape(3 * tokens, heads, size))

    def send(blocks, k, axis):
        return lax.ppermute(blocks[k], axis, [(i, i ^ k) for i in range(len(blocks))])

    blocks = list(packed)
    w_flat = w_out.reshape(wide, wide_d)
    length = n * tokens

    def attend(groups, tiles, carried, earlier=None, parts=()):
        count = len(tiles)
        carried = carried or [momentum.reshape(wide, wide_d)]
        first = len(carried) == 1
        operands = [tile_mask, *tiles, w_flat, *blocks, *carried, *parts]
        sums = shape((length, wide), F32)
        rows = shape((count * tokens, wide), BF16)
        probs = shape((heads_here, tokens, length), F32)
        scratch = [
            pltpu.VMEM((n, *packed_shape), BF16),
            pltpu.VMEM(rows.shape, BF16),
            pltpu.VMEM((count * tokens, wide_d), BF16),
            pltpu.VMEM((wide, wide_d), BF16),
            pltpu.VMEM(sums.shape, F32),
            pltpu.VMEM(sums.shape, F32),
            pltpu.SemaphoreType.DMA((count + 8 + 2 * n + wide_d // math.gcd(wide_d, 512),)),
        ]
        outs = [rows, sums, sums, rows]
        if earlier is not None:
            outs[0] = shape((n, tokens, wide), BF16)
        out_specs = [vmem] * len(outs)
        if first:
            outs += [probs, shape((tokens, wide), BF16), shape((wide, wide_d), F32)]
            out_specs += [vmem, vmem, anywhere]
            scratch += [pltpu.VMEM((wide, wide_d), F32)]
        flops = count * (14 * tokens * length * wide + 2 * tokens * wide * wide_d)
        return pl.pallas_call(
            functools.partial(
                attend_kernel, n, heads_here, per_group, groups, first, earlier, False
            ),
            in_specs=[smem] + [anywhere] * (len(operands) - 1),
            out_specs=out_specs,
            out_shape=outs,
            scratch_shapes=scratch,
            compiler_params=params(LARGE),
            cost_estimate=cost(flops, count * 2**23),
            name="attend",
        )(*operands)

    waves = waves_of(n)
    early = [[0]] + [[-s, s] for s in range(1, len(waves) + 1)]
    early_tiles, fore, aft = [own], own, own
    for wave in waves:
        fore, aft, *got = lax.optimization_barrier(
            [forward(fore), backward(aft), *[send(packed, k, "seq") for k in wave]]
        )
        early_tiles += [fore, aft]
        for k, block in zip(wave, got):
            blocks[k] = block

    groups, fresh, sums, queries, listed, atts, tiles = early, early_tiles, [], [], [], [], []
    for s in range(len(waves), half):
        if s < half - 1:
            next_fore, next_aft = forward(fore), backward(aft)
            gather = ()
        else:
            far = forward(fore)
            gather = (listed, queries)
        query, key_sum, value_sum, att, *saved = attend(groups, fresh, sums, *gather)
        sums = [key_sum, value_sum]
        if saved:
            far_probs, far_att, part = saved
        else:
            atts.append(att)
            tiles += fresh
        if s < half - 1:
            fore, aft, query, *sums = lax.optimization_barrier(
                [next_fore, next_aft, query, *sums]
            )
            listed.append(sum(groups, []))
            queries.append(query)
            groups, fresh = [[-(s + 1), s + 1]], [fore, aft]
    query_back = lax.all_to_all(query, "seq", split_axis=0, concat_axis=0, tiled=True)
    tile_count = len(tiles)
    rows = (tokens, wide)
    probs_shape = far_probs.shape
    tail_in = [tile_mask, far, w_flat, *blocks, *sums, far_probs, far_att, *atts, *tiles, part]
    far_query, grads, error, *sent = pl.pallas_call(
        functools.partial(tail_kernel, n, heads_here, per_group, workers, tile_count),
        in_specs=[smem] + [anywhere] * (len(tail_in) - 1),
        out_specs=[vmem] + [anywhere] * (2 + workers),
        out_shape=[
            shape(rows, BF16),
            shape((n, 2 * tokens, wide), BF16),
            shape((wide, wide_d), F32),
            *[shape((heads_here, size // workers, wide_d), BF16)] * workers,
        ],
        scratch_shapes=[
            pltpu.VMEM((heads_here, size, wide_d), BF16),
            pltpu.VMEM((tile_count * tokens, wide), BF16),
            pltpu.VMEM((tile_count * tokens, wide_d), BF16),
            pltpu.VMEM((wide, wide_d), F32),
            pltpu.VMEM((wide, wide_d), F32),
            pltpu.SemaphoreType.DMA((2 * tile_count + heads_here * (workers + 2),)),
            pltpu.VMEM((n, *packed_shape), BF16),
            pltpu.VMEM(rows, BF16),
            pltpu.VMEM((tokens, wide_d), BF16),
            pltpu.VMEM((wide, wide_d), BF16),
            pltpu.VMEM((length, wide), F32),
            pltpu.VMEM((length, wide), F32),
            pltpu.SemaphoreType.DMA((n + 8 + heads_here,)),
            pltpu.VMEM(probs_shape, F32),
            pltpu.VMEM(rows, BF16),
            pltpu.VMEM((n, 2 * tokens, wide), BF16),
        ],
        compiler_params=params(LARGE),
        cost_estimate=cost(HEAVY[2], 2**24),
        name="tail",
    )(*tail_in)
    across = [(ring[i], ring[(i + half) % n]) for i in range(n)]
    far_back = lax.ppermute(far_query, "seq", across)
    other_back = lax.all_to_all(grads, "seq", split_axis=0, concat_axis=0, tiled=True)

    received = [sent[0]] + [None] * (workers - 1)
    for k in range(workers - 1, 0, -1):
        received[k] = send(sent, k, "dp")

    query_back, far_back, *received = lax.optimization_barrier(
        [query_back, far_back, *received]
    )
    synced, server_error = pl.pallas_call(
        functools.partial(server_kernel, workers),
        out_shape=[
            shape((heads_here, size // workers, wide_d), BF16),
            shape((heads_here, size // workers, wide_d), F32),
        ],
        compiler_params=params(SMALL),
        cost_estimate=cost(HEAVY[0], 2**22),
        name="server",
    )(*received)
    gathered = [synced] + [None] * (workers - 1)
    for k in range(1, workers):
        source, step = (synced, k) if k == 1 or k % 2 == 0 else (gathered[k - 1], 1)
        gathered[k] = lax.ppermute(source, "dp", [(i, i ^ step) for i in range(workers)])

    grad_rows = pl.pallas_call(
        functools.partial(unpack_kernel, n),
        out_shape=shape((3 * tokens, heads, size), BF16),
        in_specs=[anywhere] * 3,
        out_specs=anywhere,
        scratch_shapes=[
            pltpu.VMEM((n, *packed_shape), BF16),
            pltpu.VMEM((tokens, wide), BF16),
            pltpu.VMEM((3 * tokens, heads, size), BF16),
            pltpu.SemaphoreType.DMA((7,)),
        ],
        compiler_params=params(SMALL),
        cost_estimate=cost(0, 4 * qkv.size),
        name="unpack",
    )(query_back, far_back, other_back)
    synced_momentum = pl.pallas_call(
        functools.partial(join_kernel, workers),
        out_shape=shape((heads_here, size, wide_d), BF16),
        compiler_params=params(SMALL),
        cost_estimate=cost(0, 4 * w_out.size),
        name="join",
    )(*gathered)
    return (
        grad_rows.reshape(qkv.shape),
        synced_momentum,
        error.reshape(1, heads_here, size, wide_d),
        server_error,
    )


def solution(mesh):
    placed = (
        P(None, "dp", "seq", None, None),
        P(),
        P("dp", "seq", None),
        P("seq", None, None),
        P("seq", None, None),
    )
    return jax.shard_map(
        body,
        mesh=mesh,
        in_specs=placed,
        out_specs=(
            P(None, "dp", "seq", None, None),
            P("seq", None, None),
            P("dp", "seq", None, None),
            P("seq", "dp", None),
        ),
        check_vma=False,
    )
```
